256 devices in a mesh: dom: 32 (over z, x), coarse: 8 (over y, core).
Axes of the slice: x: 4, y: 4, z: 8, core: 2. Of those that a mesh axis runs over, the one named last changes fastest.
Arguments:
- pressure_residual: float32 [8, 8, 8, 32, 8, 128], P(None, None, None, 'dom', 'coarse'), may hold values from -6 to 6
- margin_weight: float32 [8, 8, 8, 32, 8, 128], P(None, None, None, 'dom', 'coarse'), may hold values from 0.1 to 1.9
- stiffness_diag: float32 [8, 8, 8, 32, 8, 128], P(None, None, None, 'dom', 'coarse'), may hold values from 0.5 to 4
- fdm_basis: float32 [3, 10, 10, 32, 8, 128], P(None, None, None, 'dom', 'coarse'), may hold values from -2 to 2
- fdm_eigen: float32 [3, 10, 32, 8, 128], P(None, None, 'dom', 'coarse'), may hold values from 0.3 to 30
- coarse_map: int32 [32, 8, 128], P('dom', 'coarse'), may hold values from 0 to 127
- factor_own: float32 [32, 8, 128, 128], P('dom', 'coarse'), may hold values from -0.5 to 0.5
- factor_group: float32 [32, 8, 128, 256], P('dom', 'coarse'), may hold values from -0.125 to 0.125
- factor_top: float32 [32, 8, 128, 512], P('dom', 'coarse'), may hold values from -0.0625 to 0.0625
Outputs:
- preconditioned: float32 [8, 8, 8, 32, 8, 128], P(None, None, None, 'dom', 'coarse')
The draws below stay inside these ranges and needn't reach their ends.
All inputs are finite; a program needn't handle non-finite values.
Results may differ from the reference program's by a relative error of at most 0.000059.
Values sent between devices are 32-bit elements; how exact they have to be, the bound alone decides.
No kernel may reach another device: no remote copies, remote signals or barrier semaphores. Data moves between devices by JAX's collectives and lax.ppermute only.
A program may use at most 64 MiB of HBM per device.

```python
import math
import jax
import jax.numpy as jnp
from jax import lax

P_SIZE = 8
EP = 10
BZ = 1
BX = 1
BY = 128
CV = 128
G = 256
H = 512
NZE = 32
NXE = 8
N_DOM = 32
N_COARSE = 8


def plant(values, own_key, least, largest):
    spot = [jax.random.randint(jax.random.fold_in(own_key, axis), (), 0, length) for axis, length in enumerate(values.shape)]
    longest = values.shape.index(max(values.shape))
    next_to = spot[:longest] + [(spot[longest] + 1) % values.shape[longest]] + spot[longest + 1:]
    return values.at[tuple(spot)].set(least).at[tuple(next_to)].set(largest)


def levels(own_key, extent, shards, low, high):
    factor_of, own = 1.0, jax.random.fold_in(own_key, 6)
    for axis_at, shards_of in shards:
        steps = jnp.exp(jax.random.uniform(jax.random.fold_in(own, axis_at), (shards_of,), jnp.float32, low / len(shards), high / len(shards)))
        factor_of = factor_of * jnp.repeat(steps, extent[axis_at] // shards_of).reshape([-1 if axis == axis_at else 1 for axis in range(len(extent))])
    return factor_of


def noise(own_key, shape, width, bound, split=(), held_as=jnp.bfloat16):
    loudness = levels(own_key, shape, split, -0.22, 0.18) if split else 1.0
    array = jax.random.normal(own_key, shape, jnp.float32) * width * loudness
    return jnp.minimum(jnp.maximum(array, -bound), bound).astype(held_as)


def setup_inputs(seed: int = 0) -> dict:
    key_of = jax.random.split(jax.random.key(seed), 10)
    return {
        "pressure_residual": noise(key_of[0], (P_SIZE, P_SIZE, P_SIZE, NZE, NXE, BY), 1.0, 6.0, ((3, 32), (4, 8)), jnp.float32),
        "margin_weight": jnp.clip(1.0 + 0.18 * jax.random.normal(key_of[1], (P_SIZE, P_SIZE, P_SIZE, NZE, NXE, BY), jnp.float32), 0.1, 1.9),
        "stiffness_diag": jnp.clip(jnp.exp(math.log(4.0) - 2.0794415 * jax.random.uniform(key_of[2], (P_SIZE, P_SIZE, P_SIZE, NZE, NXE, BY), jnp.float32) ** levels(key_of[2], (P_SIZE, P_SIZE, P_SIZE, NZE, NXE, BY), ((3, 32), (4, 8)), -0.2, 0.2)), 0.5, 4.0),
        "fdm_basis": noise(key_of[3], (3, EP, EP, NZE, NXE, BY), EP ** -0.5, 2.0, ((3, 32), (4, 8)), jnp.float32),
        "fdm_eigen": jnp.clip(jnp.exp(math.log(30.0) - 4.6051701 * jax.random.uniform(key_of[4], (3, EP, NZE, NXE, BY), jnp.float32) ** levels(key_of[4], (3, EP, NZE, NXE, BY), ((2, 32), (3, 8)), -0.2, 0.2)), 0.3, 30.0),
        "coarse_map": plant(jax.random.randint(key_of[5], (NZE, NXE, BY), 0, CV), jax.random.fold_in(key_of[5], 1), 0, CV - 1).astype(jnp.int32),
        "factor_own": noise(key_of[6], (N_DOM, N_COARSE, CV, CV), CV ** -0.5, 0.5, ((0, 32), (1, 8)), jnp.float32),
        "factor_group": noise(key_of[7], (N_DOM, N_COARSE, CV, G), (16 * CV) ** -0.5, 0.125, ((0, 32), (1, 8)), jnp.float32),
        "factor_top": noise(key_of[8], (N_DOM, N_COARSE, CV, H), (64 * CV) ** -0.5, 0.0625, ((0, 32), (1, 8)), jnp.float32),
    }


sum_scale = 0.015625


def shift_zero(array_in, offset, axis):
    zero_row = jnp.zeros_like(lax.slice_in_dim(array_in, 0, 1, axis=axis))
    if offset > 0:
        return jnp.concatenate([zero_row, lax.slice_in_dim(array_in, 0, array_in.shape[axis] - 1, axis=axis)], axis=axis)
    return jnp.concatenate([lax.slice_in_dim(array_in, 1, array_in.shape[axis], axis=axis), zero_row], axis=axis)


def assemble(weighted, z_low, z_high, x_low, x_high, y_low, y_high):
    points = weighted.shape[0] + 2
    extended = jnp.zeros((points, points, points) + weighted.shape[3:], jnp.float32)
    extended = extended.at[1:-1, 1:-1, 1:-1].set(weighted)
    extended = extended.at[0, 1:-1, 1:-1].set(z_low).at[-1, 1:-1, 1:-1].set(z_high)
    extended = extended.at[1:-1, 0, 1:-1].set(x_low).at[1:-1, -1, 1:-1].set(x_high)
    extended = extended.at[1:-1, 1:-1, 0].set(y_low).at[1:-1, 1:-1, -1].set(y_high)
    return extended


def fdm_solve(extended, basis, eigen):
    best = lax.Precision.HIGHEST
    temp = jnp.einsum('akzxy,abczxy->kbczxy', basis[0], extended, precision=best)
    temp = jnp.einsum('bizxy,kbczxy->kiczxy', basis[1], temp, precision=best)
    temp = jnp.einsum('cjzxy,kiczxy->kijzxy', basis[2], temp, precision=best)
    denom = eigen[0][:, None, None] + eigen[1][None, :, None] + eigen[2][None, None, :]
    temp = temp / denom
    temp = jnp.einsum('akzxy,kijzxy->aijzxy', basis[0], temp, precision=best)
    temp = jnp.einsum('bizxy,aijzxy->abjzxy', basis[1], temp, precision=best)
    return jnp.einsum('cjzxy,abjzxy->abczxy', basis[2], temp, precision=best)


def schwarz_pass(field, margin_weight, fdm_basis, fdm_eigen):
    weighted = margin_weight * field
    z_low = jnp.roll(weighted[-1], 1, axis=2)
    z_high = jnp.roll(weighted[0], -1, axis=2)
    x_low = shift_zero(weighted[:, -1], 1, 3)
    x_high = shift_zero(weighted[:, 0], -1, 3)
    y_low = jnp.roll(weighted[:, :, -1], 1, axis=4)
    y_high = jnp.roll(weighted[:, :, 0], -1, axis=4)
    extended = assemble(weighted, z_low, z_high, x_low, x_high, y_low, y_high)
    solved = fdm_solve(extended, fdm_basis, fdm_eigen)
    result = solved[1:-1, 1:-1, 1:-1]
    result = result.at[-1].add(jnp.roll(solved[0, 1:-1, 1:-1], -1, axis=2))
    result = result.at[0].add(jnp.roll(solved[-1, 1:-1, 1:-1], 1, axis=2))
    result = result.at[:, -1].add(shift_zero(solved[1:-1, 0, 1:-1], -1, 3))
    result = result.at[:, 0].add(shift_zero(solved[1:-1, -1, 1:-1], 1, 3))
    result = result.at[:, :, -1].add(jnp.roll(solved[1:-1, 1:-1, 0], -1, axis=4))
    result = result.at[:, :, 0].add(jnp.roll(solved[1:-1, 1:-1, -1], 1, axis=4))
    return result, weighted


def reference(pressure_residual, margin_weight, stiffness_diag, fdm_basis, fdm_eigen, coarse_map, factor_own, factor_group, factor_top):
    best = lax.Precision.HIGHEST
    first, weighted = schwarz_pass(pressure_residual, margin_weight, fdm_basis, fdm_eigen)
    second, unused_weighted = schwarz_pass(pressure_residual - stiffness_diag * first, margin_weight, fdm_basis, fdm_eigen)
    schwarz = first + second
    element_sum = jnp.sum(weighted, axis=(0, 1, 2)) * sum_scale
    dom_index = (jnp.arange(NZE, dtype=jnp.int32) // BZ)[:, None, None]
    group_index = (jnp.arange(NXE, dtype=jnp.int32) // BX)[None, :, None]
    global_index = ((dom_index * N_COARSE + group_index) * CV + coarse_map).astype(jnp.int32)
    coarse_rhs = jax.ops.segment_sum(element_sum.reshape(-1), global_index.reshape(-1), num_segments=N_DOM * N_COARSE * CV)
    coarse_rhs = coarse_rhs.reshape(N_DOM, N_COARSE, CV)
    own_part = jnp.einsum('dcvj,dcv->dcj', factor_own, coarse_rhs, precision=best)
    group_part = jnp.einsum('dcvg,dcv->dg', factor_group, coarse_rhs, precision=best)
    top_part = jnp.einsum('dcvh,dcv->h', factor_top, coarse_rhs, precision=best)
    coarse_sol = jnp.einsum('dcvj,dcj->dcv', factor_own, own_part, precision=best)
    coarse_sol = coarse_sol + jnp.einsum('dcvg,dg->dcv', factor_group, group_part, precision=best)
    coarse_sol = coarse_sol + jnp.einsum('dcvh,h->dcv', factor_top, top_part, precision=best)
    correction = coarse_sol.reshape(-1)[global_index]
    return schwarz + correction[None, None, None]
```

```python
import jax
import jax.numpy as jnp
from jax import lax
from jax.sharding import PartitionSpec as P

sum_scale = 0.015625


def swap(length, stride, odd):
    ring = length // stride
    pairs = []
    for low in range(odd, ring, 2):
        high = (low + 1) % ring
        pairs += [(low, high), (high, low)]
    return [(a * stride + r, b * stride + r) for a, b in pairs for r in range(stride)]


def within(length, group, odd):
    pairs = swap(group, 1, odd)
    return [(base + a, base + b) for base in range(0, length, group) for a, b in pairs]


def add_over(value, axis, pairs):
    return value + lax.ppermute(value, axis, pairs)


def sum_coarse(value):
    size = lax.axis_size("coarse")
    value = add_over(value, "coarse", within(size, 2, 0))
    value = add_over(value, "coarse", swap(size, 2, 0))
    return add_over(value, "coarse", swap(size, 2, 1))


def sum_dom(value):
    size = lax.axis_size("dom")
    value = add_over(value, "dom", within(size, 4, 0))
    value = add_over(value, "dom", within(size, 4, 1))
    even, odd = swap(size, 4, 0), swap(size, 4, 1)
    value = add_over(value, "dom", even)
    beside = lax.ppermute(value, "dom", odd)
    across = lax.ppermute(beside, "dom", even)
    far = lax.ppermute(across, "dom", odd)
    return value + beside + across + far


def with_halo(array, sides, width, wrap):
    for axis, dim in sides:
        size, length = (lax.axis_size(axis), array.shape[dim])
        up = [(i, (i + 1) % size) for i in range(size)]
        down = [(j, i) for i, j in up]
        last = lax.slice_in_dim(array, length - width, length, axis=dim)
        leading = lax.slice_in_dim(array, 0, width, axis=dim)
        before = lax.ppermute(last, axis, up)
        after = lax.ppermute(leading, axis, down)
        if not wrap:
            place = lax.axis_index(axis)
            before = jnp.where(place == 0, 0.0, before)
            after = jnp.where(place == size - 1, 0.0, after)
        array = jnp.concatenate([before, array, after], axis=dim)
    return array


def assemble(weighted, z_low, z_high, x_low, x_high, y_low, y_high):
    points = weighted.shape[0] + 2
    extended = jnp.zeros((points, points, points) + weighted.shape[3:], jnp.float32)
    extended = extended.at[1:-1, 1:-1, 1:-1].set(weighted)
    extended = extended.at[0, 1:-1, 1:-1].set(z_low).at[-1, 1:-1, 1:-1].set(z_high)
    extended = extended.at[1:-1, 0, 1:-1].set(x_low).at[1:-1, -1, 1:-1].set(x_high)
    extended = extended.at[1:-1, 1:-1, 0].set(y_low).at[1:-1, 1:-1, -1].set(y_high)
    return extended


def contract(basis_one, source, axis, forward):
    total = None
    others = tuple((dim for dim in range(3) if dim != axis))
    for index in range(source.shape[axis]):
        if forward:
            coef = basis_one[index]
        else:
            coef = basis_one[:, index]
        coef = jnp.expand_dims(coef, others)
        piece = lax.slice_in_dim(source, index, index + 1, axis=axis)
        term = coef * piece
        total = term if total is None else total + term
    return total


def fdm_solve(extended, basis, eigen):
    temp = contract(basis[0], extended, 0, True)
    temp = contract(basis[1], temp, 1, True)
    temp = contract(basis[2], temp, 2, True)
    denom = eigen[0][:, None, None] + eigen[1][None, :, None] + eigen[2][None, None, :]
    temp = temp / denom
    temp = contract(basis[0], temp, 0, False)
    temp = contract(basis[1], temp, 1, False)
    return contract(basis[2], temp, 2, False)


def schwarz_pass(field, margin_weight, fdm_basis, fdm_eigen):
    weighted = margin_weight * field
    z_faces = jnp.stack([weighted[0, :, :, 0], weighted[-1, :, :, -1]])
    z_halo = with_halo(z_faces, (("dom", 0),), 1, True)
    x_faces = jnp.stack([weighted[:, 0, :, :, 0], weighted[:, -1, :, :, -1]])
    x_halo = with_halo(x_faces, (("coarse", 0),), 1, False)
    z_low_rest = weighted[-1, :, :, :-1]
    z_high_rest = weighted[0, :, :, 1:]
    x_low_rest = weighted[:, -1, :, :, :-1]
    x_high_rest = weighted[:, 0, :, :, 1:]
    y_low = jnp.roll(weighted[:, :, -1], 1, axis=4)
    y_high = jnp.roll(weighted[:, :, 0], -1, axis=4)
    z_low_recv = z_halo[0][:, :, None]
    z_high_recv = z_halo[3][:, :, None]
    x_low_recv = x_halo[0][:, :, :, None]
    x_high_recv = x_halo[3][:, :, :, None]
    extended = assemble(
        weighted,
        jnp.concatenate([z_low_recv, z_low_rest], axis=2),
        jnp.concatenate([z_high_rest, z_high_recv], axis=2),
        jnp.concatenate([x_low_recv, x_low_rest], axis=3),
        jnp.concatenate([x_high_rest, x_high_recv], axis=3),
        y_low,
        y_high,
    )
    solved = fdm_solve(extended, fdm_basis, fdm_eigen)
    result = solved[1:-1, 1:-1, 1:-1]
    z_back = jnp.stack([solved[0, 1:-1, 1:-1, 0], solved[-1, 1:-1, 1:-1, -1]])
    z_recv = with_halo(z_back, (("dom", 0),), 1, True)
    result = result.at[-1].add(
        jnp.concatenate([solved[0, 1:-1, 1:-1, 1:], z_recv[3][:, :, None]], axis=2)
    )
    result = result.at[0].add(
        jnp.concatenate([z_recv[0][:, :, None], solved[-1, 1:-1, 1:-1, :-1]], axis=2)
    )
    x_back = jnp.stack([solved[1:-1, 0, 1:-1, :, 0], solved[1:-1, -1, 1:-1, :, -1]])
    x_recv = with_halo(x_back, (("coarse", 0),), 1, False)
    result = result.at[:, -1].add(
        jnp.concatenate([solved[1:-1, 0, 1:-1, :, 1:], x_recv[3][:, :, :, None]], axis=3)
    )
    result = result.at[:, 0].add(
        jnp.concatenate([x_recv[0][:, :, :, None], solved[1:-1, -1, 1:-1, :, :-1]], axis=3)
    )
    result = result.at[:, :, -1].add(jnp.roll(solved[1:-1, 1:-1, 0], -1, axis=4))
    result = result.at[:, :, 0].add(jnp.roll(solved[1:-1, 1:-1, -1], 1, axis=4))
    return result


def coarse_solve(weighted, coarse_map, factor_own, factor_group, factor_top):
    best = lax.Precision.HIGHEST
    unknowns = factor_own.shape[2]
    element_sum = jnp.sum(weighted, axis=(0, 1, 2)) * sum_scale
    one_hot = (
        coarse_map.reshape(-1)[:, None] == jnp.arange(unknowns, dtype=jnp.int32)[None, :]
    ).astype(jnp.float32)
    coarse_rhs = jnp.dot(element_sum.reshape(1, -1), one_hot, precision=best)[0]
    own_block = factor_own[0, 0]
    group_block = factor_group[0, 0]
    top_block = factor_top[0, 0]
    own_part = jnp.dot(coarse_rhs, own_block, precision=best)
    group_term = jnp.dot(coarse_rhs, group_block, precision=best)
    top_term = jnp.dot(coarse_rhs, top_block, precision=best)
    both = sum_coarse(jnp.concatenate([group_term, top_term]).reshape(-1, 128))
    group_part = both[: group_term.shape[0] // 128].reshape(-1)
    top_part = sum_dom(both[group_term.shape[0] // 128 :]).reshape(-1)
    coarse_sol = jnp.dot(own_block, own_part, precision=best)
    coarse_sol = coarse_sol + jnp.dot(group_block, group_part, precision=best)
    coarse_sol = coarse_sol + jnp.dot(top_block, top_part, precision=best)
    correction = jnp.dot(one_hot, coarse_sol, precision=best)
    return correction.reshape(coarse_map.shape)


def body(
    pressure_residual,
    margin_weight,
    stiffness_diag,
    fdm_basis,
    fdm_eigen,
    coarse_map,
    factor_own,
    factor_group,
    factor_top,
):
    first = schwarz_pass(pressure_residual, margin_weight, fdm_basis, fdm_eigen)
    second = schwarz_pass(
        pressure_residual - stiffness_diag * first, margin_weight, fdm_basis, fdm_eigen
    )
    correction = coarse_solve(
        margin_weight * pressure_residual, coarse_map, factor_own, factor_group, factor_top
    )
    return first + second + correction[None, None, None]


def solution(mesh):
    in_specs = (
        P(None, None, None, "dom", "coarse", None),
        P(None, None, None, "dom", "coarse", None),
        P(None, None, None, "dom", "coarse", None),
        P(None, None, None, "dom", "coarse", None),
        P(None, None, "dom", "coarse", None),
        P("dom", "coarse", None),
        P("dom", "coarse", None, None),
        P("dom", "coarse", None, None),
        P("dom", "coarse", None, None),
    )
    out_specs = P(None, None, None, "dom", "coarse", None)
    return jax.shard_map(body, mesh=mesh, in_specs=in_specs, out_specs=out_specs, check_vma=False)
```

```python
import jax
import jax.numpy as jnp
from jax import lax
from jax.experimental import pallas as pl
from jax.experimental.pallas import tpu as pltpu
from jax.sharding import PartitionSpec as P

sum_scale = 0.015625
F32 = jnp.float32
FACE = 64
LINK = 144
VMEM = pl.BlockSpec(memory_space=pltpu.VMEM)


def swap(length, stride, odd):
    ring = length // stride
    pairs = []
    for low in range(odd, ring, 2):
        high = (low + 1) % ring
        pairs += [(low, high), (high, low)]
    return [(a * stride + r, b * stride + r) for a, b in pairs for r in range(stride)]


def within(length, group, odd):
    pairs = swap(group, 1, odd)
    return [(base + a, base + b) for base in range(0, length, group) for a, b in pairs]


def call(kernel, out_rows, scratch_rows, *args):
    flops = 2 * 60000 * 128 if scratch_rows else 200000
    return pl.pallas_call(
        kernel,
        out_shape=[jax.ShapeDtypeStruct((rows, 128), F32) for rows in out_rows],
        in_specs=[pl.BlockSpec(memory_space=pltpu.SMEM) if a.ndim == 1 else VMEM for a in args],
        out_specs=[VMEM] * len(out_rows),
        scratch_shapes=[pltpu.VMEM((rows, 128), F32) for rows in scratch_rows],
        compiler_params=pltpu.CompilerParams(vmem_limit_bytes=8 * 1024 * 1024),
        cost_estimate=pl.CostEstimate(flops=flops, bytes_accessed=1000000, transcendentals=0),
    )(*args)


def rows8(start):
    return pl.ds(pl.multiple_of(start, 8), 8)


def every(start, stride):
    return pl.ds(start, 8, stride=stride)


def weigh(basis, direction, inputs, first_in, outs, forward):
    results = []
    for out in outs:
        total = None
        for at, tiles in enumerate(inputs):
            pair = (first_in + at, out) if forward else (out, first_in + at)
            coef = basis[pl.ds(direction * 100 + pair[0] * 10 + pair[1], 1), :]
            terms = [coef * tile for tile in tiles]
            total = terms if total is None else [a + b for a, b in zip(total, terms)]
        results.append(total)
    return results


def solve(field, z_low, z_high, x_low, x_high, basis, eigen, out, z0, z9, x0, x9, work, plane, ylow, yhigh, zx):
    all_ten = range(10)
    inner = range(1, 9)

    def y_face_in(face, at, turn):
        lines = [[pltpu.roll(field[every(k * 64 + at, 8), :], turn, 1)] for k in range(8)]
        for k, (value,) in enumerate(weigh(basis, 0, lines, 1, all_ten, True)):
            plane[rows8(k * 8), :] = value
        lines = [[plane[every(i, 8), :], plane[every(64 + i, 8), :]] for i in range(8)]
        for i, (value, rest) in enumerate(weigh(basis, 1, lines, 1, all_ten, True)):
            face[every(i, 10), :] = value
            face[every(80 + i, 10), :] = rest

    y_face_in(ylow, 7, 1)
    y_face_in(yhigh, 0, 127)

    def forward_z(step, carry):
        tiles = [step * 2, step * 2 + 1]
        lines = [[z_low[rows8(i * 8), :] for i in tiles]]
        lines += [[field[rows8(k * 64 + i * 8), :] for i in tiles] for k in range(8)]
        lines += [[z_high[rows8(i * 8), :] for i in tiles]]
        for k, values in enumerate(weigh(basis, 0, lines, 0, all_ten, True)):
            for i, value in zip(tiles, values):
                work[rows8((k * 10 + i + 1) * 8), :] = value
        return carry

    lax.fori_loop(0, 4, forward_z, 0)
    lines = [[x_low[rows8(k * 8), :], x_high[rows8(k * 8), :]] for k in range(8)]
    for k, (low, high) in enumerate(weigh(basis, 0, lines, 1, all_ten, True)):
        work[rows8(k * 80), :] = low
        work[rows8(k * 80 + 72), :] = high

    def turn_x(forward):
        def step_x(step, carry):
            ks = [step * 2, step * 2 + 1]
            lines = [[work[rows8(k * 80 + i * 8), :] for k in ks] for i in range(10)]
            for i, values in enumerate(weigh(basis, 1, lines, 0, all_ten, forward)):
                for k, value in zip(ks, values):
                    work[rows8(k * 80 + i * 8), :] = value
            return carry

        lax.fori_loop(0, 5, step_x, 0)

    turn_x(True)
    for k in range(10):
        zx[pl.ds(k * 10, 10), :] = eigen[pl.ds(k, 1), :] + eigen[pl.ds(10, 10), :]

    def step_y(step, carry):
        rows = rows8(step * 8)
        lines = [[ylow[rows, :]]] + [[work[every(step * 64 + j, 8), :]] for j in range(8)] + [[yhigh[rows, :]]]
        spectral = weigh(basis, 2, lines, 0, all_ten, True)
        sums = zx[rows, :]
        spectral = [[value / (sums + eigen[pl.ds(20 + j, 1), :])] for j, (value,) in enumerate(spectral)]
        solved = weigh(basis, 2, spectral, 0, all_ten, False)
        ylow[rows, :] = solved[0][0]
        yhigh[rows, :] = solved[9][0]
        for j in range(8):
            work[every(step * 64 + j, 8), :] = solved[j + 1][0]
        return carry

    lax.fori_loop(0, 13, step_y, 0)
    turn_x(False)

    def back_z(step, carry):
        tiles = [step * 2, step * 2 + 1]
        lines = [[work[rows8((k * 10 + i + 1) * 8), :] for i in tiles] for k in range(10)]
        for k, values in enumerate(weigh(basis, 0, lines, 0, all_ten, False)):
            for i, value in zip(tiles, values):
                if k == 0:
                    z0[rows8(i * 8), :] = value
                elif k == 9:
                    z9[rows8(i * 8), :] = value
                else:
                    out[rows8((k - 1) * 64 + i * 8), :] = value
        return carry

    lax.fori_loop(0, 4, back_z, 0)
    lines = [[work[rows8(k * 80), :], work[rows8(k * 80 + 72), :]] for k in range(10)]
    for k, (low, high) in enumerate(weigh(basis, 0, lines, 0, inner, False)):
        x0[rows8(k * 8), :] = low
        x9[rows8(k * 8), :] = high

    def y_face_out(face, at, turn):
        lines = [[face[every(i, 10), :], face[every(80 + i, 10), :]] for i in range(10)]
        for i, (value, rest) in enumerate(weigh(basis, 1, lines, 0, inner, False)):
            plane[rows8(i * 16), :] = value
            plane[rows8(i * 16 + 8), :] = rest
        lines = [[plane[every(k, 16), :]] for k in range(10)]
        for k, (value,) in enumerate(weigh(basis, 0, lines, 0, inner, False)):
            out[every(k * 64 + at, 8), :] += pltpu.roll(value, turn, 1)

    y_face_out(ylow, 7, 127)
    y_face_out(yhigh, 0, 1)


SOLVE_SCRATCH = (840, 128, 160, 160, 104)


def layer(k):
    return pl.ds(k * 64, 64)


def put_x(ref, base, array, i):
    for k in range(8):
        ref[pl.ds(base + k * 8, 8), :] = array[pl.ds(k * 64 + i * 8, 8), :]


def pick(flag, array, other, start, rows):
    return jnp.where(flag, array[pl.ds(start, rows), :], other[pl.ds(start, rows), :])


def hand_out(flag, up, down, even, odd):
    even[...] = jnp.where(flag, up[...], down[...])
    odd[...] = jnp.where(flag, down[...], up[...])


def pre_kernel(place, residual, margin, diag, w, c2, ze, zo, xe, xo, zu, zd, xu, xd):
    w[...] = margin[...] * residual[...]
    c2[...] = margin[...] * diag[...]
    for base, source in ((0, w), (FACE, c2)):
        zu[pl.ds(base, FACE), :] = source[layer(7), :]
        zd[pl.ds(base, FACE), :] = source[layer(0), :]
        put_x(xu, base, source, 7)
        put_x(xd, base, source, 0)
    hand_out(place[0] == 0, zu, zd, ze, zo)
    hand_out(place[1] == 0, xu, xd, xe, xo)


def coarse_kernel(w, coarse_map, own, group, top, terms, own_part):
    total = w[pl.ds(0, 8), :]
    for at in range(8, 512, 8):
        total = total + w[pl.ds(at, 8), :]
    element_sum = jnp.sum(total, axis=0, keepdims=True) * sum_scale
    hit = lax.broadcasted_iota(jnp.int32, (128, 128), 0) == coarse_map[pl.ds(0, 1), :]
    rhs = jnp.sum(jnp.where(hit, element_sum, 0.0), axis=1, keepdims=True)
    own_part[...] = jnp.zeros((8, 128), F32)
    own_part[pl.ds(0, 1), :] = jnp.sum(own[...] * rhs, axis=0, keepdims=True)
    terms[...] = jnp.zeros((8, 128), F32)
    for at in range(4):
        terms[pl.ds(at, 1), :] = jnp.sum(top[:, at * 128 : (at + 1) * 128] * rhs, axis=0, keepdims=True)
    for at in range(2):
        terms[pl.ds(4 + at, 1), :] = jnp.sum(group[:, at * 128 : (at + 1) * 128] * rhs, axis=0, keepdims=True)


def correct_kernel(total, grouped, own_part, coarse_map, own, group, top, correction):
    sums = own[...] * own_part[pl.ds(0, 1), :]
    for at in range(2):
        sums = sums + group[:, at * 128 : (at + 1) * 128] * grouped[pl.ds(4 + at, 1), :]
    for at in range(4):
        sums = sums + top[:, at * 128 : (at + 1) * 128] * total[pl.ds(at, 1), :]
    sol = jnp.sum(sums, axis=1, keepdims=True)
    hit = lax.broadcasted_iota(jnp.int32, (128, 128), 0) == coarse_map[pl.ds(0, 1), :]
    correction[...] = jnp.zeros((8, 128), F32)
    correction[pl.ds(0, 1), :] = jnp.sum(jnp.where(hit, sol, 0.0), axis=0, keepdims=True)


def first_kernel(place, w, c2, ze, zo, xe, xo, basis, eigen, r, z0, z9, x0, x9, oe, oo, zl, zh, xl, xh, xu, xd, *work):
    z_low = place[0] == 0
    x_low = place[1] == 0
    zh[...] = pick(z_low, ze, zo, 0, FACE)
    zl[...] = pick(z_low, zo, ze, 0, FACE)
    xh[...] = jnp.where(place[3] == 1, pick(x_low, xe, xo, 0, FACE), 0.0)
    xl[...] = jnp.where(place[2] == 1, pick(x_low, xo, xe, 0, FACE), 0.0)
    solve(w, zl, zh, xl, xh, basis, eigen, r, z0, z9, x0, x9, *work)
    for message, face, i in ((xu, x9, 7), (xd, x0, 0)):
        message[pl.ds(0, FACE), :] = face[...]
        for k in range(8):
            here = pl.ds(k * 64 + i * 8, 8)
            message[pl.ds(FACE + k * 8, 8), :] = w[here, :] - c2[here, :] * r[here, :]
        message[pl.ds(128, 8), :] = z9[pl.ds(i * 8, 8), :]
        message[pl.ds(136, 8), :] = z0[pl.ds(i * 8, 8), :]
    hand_out(x_low, xu, xd, oe, oo)


def middle_kernel(place, r, w, c2, z0, z9, xe, xo, r2, ze, zo, zu, zd):
    x_low = place[1] == 0
    above = jnp.where(place[3] == 1, pick(x_low, xe, xo, 0, LINK), 0.0)
    below = jnp.where(place[2] == 1, pick(x_low, xo, xe, 0, LINK), 0.0)
    r2[...] = r[...]
    for k in range(8):
        r2[pl.ds(k * 64 + 56, 8), :] += above[k * 8 : k * 8 + 8]
        r2[pl.ds(k * 64, 8), :] += below[k * 8 : k * 8 + 8]
    for message, face, k, edge in ((zu, z9, 7, 128), (zd, z0, 0, 136)):
        message[pl.ds(0, FACE), :] = face[...]
        message[pl.ds(FACE, FACE), :] = w[layer(k), :] - c2[layer(k), :] * r2[layer(k), :]
        message[pl.ds(128, 8), :] = below[edge : edge + 8]
        message[pl.ds(136, 8), :] = above[edge : edge + 8]
    hand_out(place[0] == 0, zu, zd, ze, zo)


def second_kernel(
    place, r2, w, c2, z0, z9, x0, x9, aze, azo, axe, axo, xe, xo, ze, zo, basis, eigen,
    first, ce, co, de, do, field, out, zl, zh, xl, xh, s0, s9, t0, t9, *work
):
    z_low = place[0] == 0
    x_low = place[1] == 0
    from_up = lambda start, rows: pick(z_low, ze, zo, start, rows)
    from_down = lambda start, rows: pick(z_low, zo, ze, start, rows)
    first[...] = r2[...]
    first[layer(7), :] += from_up(0, FACE)
    first[layer(0), :] += from_down(0, FACE)
    zh[...] = from_up(FACE, FACE) - pick(z_low, aze, azo, FACE, FACE) * z9[...]
    zl[...] = from_down(FACE, FACE) - pick(z_low, azo, aze, FACE, FACE) * z0[...]
    xh[...] = x9[...]
    xl[...] = x0[...]
    xl[pl.ds(0, 8), :] += from_down(128, 8)
    xl[pl.ds(56, 8), :] += from_up(128, 8)
    xh[pl.ds(0, 8), :] += from_down(136, 8)
    xh[pl.ds(56, 8), :] += from_up(136, 8)
    value = pick(x_low, xe, xo, FACE, FACE) - pick(x_low, axe, axo, FACE, FACE) * xh[...]
    xh[...] = jnp.where(place[3] == 1, value, 0.0)
    value = pick(x_low, xo, xe, FACE, FACE) - pick(x_low, axo, axe, FACE, FACE) * xl[...]
    xl[...] = jnp.where(place[2] == 1, value, 0.0)
    field[...] = w[...] - c2[...] * first[...]
    solve(field, zl, zh, xl, xh, basis, eigen, out, s0, s9, t0, t9, *work)
    first[...] += out[...]
    hand_out(z_low, s9, s0, ce, co)
    hand_out(x_low, t9, t0, de, do)


def last_kernel(place, first, ze, zo, xe, xo, correction, out):
    z_low = place[0] == 0
    x_low = place[1] == 0
    out[...] = first[...] + correction[pl.ds(0, 1), :]
    out[layer(7), :] += pick(z_low, ze, zo, 0, FACE)
    out[layer(0), :] += pick(z_low, zo, ze, 0, FACE)
    above = jnp.where(place[3] == 1, pick(x_low, xe, xo, 0, FACE), 0.0)
    below = jnp.where(place[2] == 1, pick(x_low, xo, xe, 0, FACE), 0.0)
    for k in range(8):
        out[pl.ds(k * 64 + 56, 8), :] += above[k * 8 : k * 8 + 8]
        out[pl.ds(k * 64, 8), :] += below[k * 8 : k * 8 + 8]


def add_over(value, axis, pairs):
    return value + lax.ppermute(value, axis, pairs)


def sum_coarse(value):
    size = lax.axis_size("coarse")
    value = add_over(value, "coarse", within(size, 2, 0))
    value = add_over(value, "coarse", swap(size, 2, 0))
    return add_over(value, "coarse", swap(size, 2, 1))


def sum_dom(value):
    size = lax.axis_size("dom")
    value = add_over(value, "dom", within(size, 4, 0))
    value = add_over(value, "dom", within(size, 4, 1))
    even, odd = swap(size, 4, 0), swap(size, 4, 1)
    value = add_over(value, "dom", even)
    beside = lax.ppermute(value, "dom", odd)
    across = lax.ppermute(beside, "dom", even)
    far = lax.ppermute(across, "dom", odd)
    return value + beside + across + far


def over(axis, even, odd):
    size = lax.axis_size(axis)
    even = lax.ppermute(even, axis, swap(size, 1, 0))
    odd = lax.ppermute(odd, axis, swap(size, 1, 1))
    return even, odd


def body(residual, margin, diag, basis, eigen, coarse_map, own, group, top):
    shape = residual.shape
    residual, margin, diag = (a.reshape(-1, 128) for a in (residual, margin, diag))
    basis, eigen, coarse_map = (a.reshape(-1, 128) for a in (basis, eigen, coarse_map))
    own, group, top = (a.reshape(128, -1) for a in (own, group, top))
    dom, coarse = lax.axis_index("dom"), lax.axis_index("coarse")
    last = lax.axis_size("coarse") - 1
    place = jnp.stack([dom % 2, coarse % 2, (coarse > 0).astype(jnp.int32), (coarse < last).astype(jnp.int32)])
    place = place.astype(jnp.int32)

    w, c2, ze, zo, xe, xo = call(pre_kernel, (512, 512) + (128,) * 4, (128,) * 4, place, residual, margin, diag)
    axe, axo = over("coarse", xe, xo)
    aze, azo = over("dom", ze, zo)
    terms, own_part = call(coarse_kernel, (8, 8), (), w, coarse_map, own, group, top)
    grouped = sum_coarse(terms)
    r, z0, z9, x0, x9, xe, xo = call(
        first_kernel, (512,) + (FACE,) * 4 + (LINK,) * 2, (FACE,) * 4 + (LINK,) * 2 + SOLVE_SCRATCH,
        place, w, c2, aze, azo, axe, axo, basis, eigen,
    )
    xe, xo = over("coarse", xe, xo)
    r2, ze, zo = call(middle_kernel, (512, LINK, LINK), (LINK,) * 2, place, r, w, c2, z0, z9, xe, xo)
    ze, zo = over("dom", ze, zo)
    total = sum_dom(grouped)
    first, ce, co, de, do = call(
        second_kernel, (512,) + (FACE,) * 4, (512, 512) + (FACE,) * 8 + SOLVE_SCRATCH,
        place, r2, w, c2, z0, z9, x0, x9, aze, azo, axe, axo, xe, xo, ze, zo, basis, eigen,
    )
    xe, xo = over("coarse", de, do)
    ze, zo = over("dom", ce, co)
    (correction,) = call(correct_kernel, (8,), (), total, grouped, own_part, coarse_map, own, group, top)
    (out,) = call(last_kernel, (512,), (), place, first, ze, zo, xe, xo, correction)
    return out.reshape(shape)


def solution(mesh):
    field = P(None, None, None, "dom", "coarse", None)
    factor = P("dom", "coarse", None, None)
    in_specs = (field, field, field, field, P(None, None, "dom", "coarse", None), P("dom", "coarse", None))
    in_specs = in_specs + (factor, factor, factor)
    return jax.shard_map(body, mesh=mesh, in_specs=in_specs, out_specs=field, check_vma=False)
```

```python
import jax
import jax.numpy as jnp
from jax import lax
from jax.experimental import pallas as pl
from jax.experimental.pallas import tpu as pltpu
from jax.sharding import PartitionSpec as P

sum_scale = 0.015625
F32 = jnp.float32
FACE = 64
LINK = 144
VMEM = pl.BlockSpec(memory_space=pltpu.VMEM)


def swap(length, stride, odd):
    ring = length // stride
    pairs = []
    for low in range(odd, ring, 2):
        high = (low + 1) % ring
        pairs += [(low, high), (high, low)]
    return [(a * stride + r, b * stride + r) for a, b in pairs for r in range(stride)]


def within(length, group, odd):
    pairs = swap(group, 1, odd)
    return [(base + a, base + b) for base in range(0, length, group) for a, b in pairs]


def call(kernel, outs, scratch_rows, *args, in_hbm=(), scratch=(), flops=2 * 60000 * 128):
    outs = [jax.ShapeDtypeStruct((out, 128), F32) if isinstance(out, int) else out for out in outs]
    specs = [pl.BlockSpec(memory_space=pltpu.SMEM) if a.ndim == 1 else VMEM for a in args]
    args = list(args)
    for at in in_hbm:
        specs[at] = pl.BlockSpec(memory_space=pltpu.HBM)
        args[at] = pltpu.with_memory_space_constraint(args[at], pltpu.HBM)
    return pl.pallas_call(
        kernel,
        out_shape=outs,
        in_specs=specs,
        out_specs=[VMEM] * len(outs),
        scratch_shapes=[pltpu.VMEM((rows, 128), F32) for rows in scratch_rows] + list(scratch),
        compiler_params=pltpu.CompilerParams(vmem_limit_bytes=8 * 1024 * 1024),
        cost_estimate=pl.CostEstimate(flops=flops, bytes_accessed=1000000, transcendentals=0),
    )(*args)


def rows8(start):
    return pl.ds(pl.multiple_of(start, 8), 8)


def every(start, stride):
    return pl.ds(start, 8, stride=stride)


def weigh(basis, direction, inputs, first_in, outs, forward):
    results = []
    for out in outs:
        total = None
        for at, tiles in enumerate(inputs):
            pair = (first_in + at, out) if forward else (out, first_in + at)
            coef = basis[direction * 100 + pair[0] * 10 + pair[1]]
            terms = [coef * tile for tile in tiles]
            total = terms if total is None else [a + b for a, b in zip(total, terms)]
        results.append(total)
    return results


def solve(field, z_low, z_high, x_low, x_high, basis, eigen, out, z0, z9, x0, x9, work, plane, ylow, yhigh, zx):
    all_ten = range(10)
    inner = range(1, 9)

    def y_face_in(face, at, turn):
        lines = [[pltpu.roll(field[every(k * 64 + at, 8), :], turn, 1)] for k in range(8)]
        for k, (value,) in enumerate(weigh(basis, 0, lines, 1, all_ten, True)):
            plane[rows8(k * 8), :] = value
        lines = [[plane[every(i, 8), :], plane[every(64 + i, 8), :]] for i in range(8)]
        for i, (value, rest) in enumerate(weigh(basis, 1, lines, 1, all_ten, True)):
            face[every(i, 10), :] = value
            face[every(80 + i, 10), :] = rest

    y_face_in(ylow, 7, 1)
    y_face_in(yhigh, 0, 127)

    def forward_z(step, carry):
        tiles = [step * 2, step * 2 + 1]
        lines = [[z_low[rows8(i * 8), :] for i in tiles]]
        lines += [[field[rows8(k * 64 + i * 8), :] for i in tiles] for k in range(8)]
        lines += [[z_high[rows8(i * 8), :] for i in tiles]]
        for k, values in enumerate(weigh(basis, 0, lines, 0, all_ten, True)):
            for i, value in zip(tiles, values):
                work[rows8((k * 10 + i + 1) * 8), :] = value
        return carry

    lax.fori_loop(0, 4, forward_z, 0)
    lines = [[x_low[rows8(k * 8), :], x_high[rows8(k * 8), :]] for k in range(8)]
    for k, (low, high) in enumerate(weigh(basis, 0, lines, 1, all_ten, True)):
        work[rows8(k * 80), :] = low
        work[rows8(k * 80 + 72), :] = high

    def turn_x(forward):
        def step_x(step, carry):
            ks = [step * 2, step * 2 + 1]
            lines = [[work[rows8(k * 80 + i * 8), :] for k in ks] for i in range(10)]
            for i, values in enumerate(weigh(basis, 1, lines, 0, all_ten, forward)):
                for k, value in zip(ks, values):
                    work[rows8(k * 80 + i * 8), :] = value
            return carry

        lax.fori_loop(0, 5, step_x, 0)

    turn_x(True)
    for k in range(10):
        for i in range(10):
            zx[pl.ds(k * 10 + i, 1), :] = eigen[k] + eigen[10 + i]

    def step_y(step, carry):
        rows = rows8(step * 8)
        lines = [[ylow[rows, :]]] + [[work[every(step * 64 + j, 8), :]] for j in range(8)] + [[yhigh[rows, :]]]
        spectral = weigh(basis, 2, lines, 0, all_ten, True)
        sums = zx[rows, :]
        spectral = [[value / (sums + eigen[20 + j])] for j, (value,) in enumerate(spectral)]
        solved = weigh(basis, 2, spectral, 0, all_ten, False)
        ylow[rows, :] = solved[0][0]
        yhigh[rows, :] = solved[9][0]
        for j in range(8):
            work[every(step * 64 + j, 8), :] = solved[j + 1][0]
        return carry

    lax.fori_loop(0, 13, step_y, 0)
    turn_x(False)

    def back_z(step, carry):
        tiles = [step * 2, step * 2 + 1]
        lines = [[work[rows8((k * 10 + i + 1) * 8), :] for i in tiles] for k in range(10)]
        for k, values in enumerate(weigh(basis, 0, lines, 0, all_ten, False)):
            for i, value in zip(tiles, values):
                if k == 0:
                    z0[rows8(i * 8), :] = value
                elif k == 9:
                    z9[rows8(i * 8), :] = value
                else:
                    out[rows8((k - 1) * 64 + i * 8), :] = value
        return carry

    lax.fori_loop(0, 4, back_z, 0)
    lines = [[work[rows8(k * 80), :], work[rows8(k * 80 + 72), :]] for k in range(10)]
    for k, (low, high) in enumerate(weigh(basis, 0, lines, 0, inner, False)):
        x0[rows8(k * 8), :] = low
        x9[rows8(k * 8), :] = high

    def y_face_out(face, at, turn):
        lines = [[face[every(i, 10), :], face[every(80 + i, 10), :]] for i in range(10)]
        for i, (value, rest) in enumerate(weigh(basis, 1, lines, 0, inner, False)):
            plane[rows8(i * 16), :] = value
            plane[rows8(i * 16 + 8), :] = rest
        lines = [[plane[every(k, 16), :]] for k in range(10)]
        for k, (value,) in enumerate(weigh(basis, 0, lines, 0, inner, False)):
            out[every(k * 64 + at, 8), :] += pltpu.roll(value, turn, 1)

    y_face_out(ylow, 7, 127)
    y_face_out(yhigh, 0, 1)


SOLVE_SCRATCH = (840, 128, 160, 160, 104)


def layer(k):
    return pl.ds(k * 64, 64)


def put_x(ref, base, array, i):
    for k in range(8):
        ref[pl.ds(base + k * 8, 8), :] = array[pl.ds(k * 64 + i * 8, 8), :]


def pick(flag, array, other, start, rows):
    return jnp.where(flag, array[pl.ds(start, rows), :], other[pl.ds(start, rows), :])


def hand_out(flag, up, down, even, odd):
    even[...] = jnp.where(flag, up[...], down[...])
    odd[...] = jnp.where(flag, down[...], up[...])


def pre_kernel(
    place, residual_hbm, margin_hbm, diag_hbm, map_hbm, own_hbm, group_hbm, top_hbm,
    xe, zo, ze, xo, w, c2, terms, own_part, coarse_map, own, group, top,
    residual, margin, diag, zu, zd, xu, xd, sems
):
    copies = [
        pltpu.make_async_copy(source, target, sems.at[at])
        for at, (source, target) in enumerate((
            (residual_hbm, residual), (margin_hbm, margin), (diag_hbm, diag), (map_hbm, coarse_map),
            (own_hbm, own), (group_hbm, group), (top_hbm, top),
        ))
    ]
    for copy in copies:
        copy.start()
    copies[0].wait()
    copies[1].wait()
    w[...] = margin[...] * residual[...]
    copies[2].wait()
    c2[...] = margin[...] * diag[...]
    for base, source in ((0, w), (FACE, c2)):
        zu[pl.ds(base, FACE), :] = source[layer(7), :]
        zd[pl.ds(base, FACE), :] = source[layer(0), :]
        put_x(xu, base, source, 7)
        put_x(xd, base, source, 0)
    z_low, x_low = place[0] == 0, place[1] == 0
    hand_out(z_low, zu, zd, ze, zo)
    xo[...] = jnp.where(x_low, xd[...], xu[...])
    xe[pl.ds(0, 128), :] = jnp.where(x_low, xu[...], xd[...])
    for copy in copies[3:]:
        copy.wait()
    total = w[pl.ds(0, 8), :]
    for at in range(8, 512, 8):
        total = total + w[pl.ds(at, 8), :]
    element_sum = jnp.sum(total, axis=0, keepdims=True) * sum_scale
    hit = lax.broadcasted_iota(jnp.int32, (128, 128), 0) == coarse_map[pl.ds(0, 1), :]
    rhs = jnp.sum(jnp.where(hit, element_sum, 0.0), axis=1, keepdims=True)
    own_part[...] = jnp.zeros((8, 128), F32)
    own_part[pl.ds(0, 1), :] = jnp.sum(own[...] * rhs, axis=0, keepdims=True)
    terms[...] = jnp.zeros((8, 128), F32)
    for at in range(4):
        terms[pl.ds(at, 1), :] = jnp.sum(top[:, at * 128 : (at + 1) * 128] * rhs, axis=0, keepdims=True)
    for at in range(2):
        terms[pl.ds(4 + at, 1), :] = jnp.sum(group[:, at * 128 : (at + 1) * 128] * rhs, axis=0, keepdims=True)
    xe[pl.ds(128, 8), :] = terms[...]


def correct(total, grouped, own_part, coarse_map, own, group, top):
    sums = own[...] * own_part[pl.ds(0, 1), :]
    for at in range(2):
        sums = sums + group[:, at * 128 : (at + 1) * 128] * grouped[4 + at : 5 + at]
    for at in range(4):
        sums = sums + top[:, at * 128 : (at + 1) * 128] * total[at : at + 1]
    sol = jnp.sum(sums, axis=1, keepdims=True)
    hit = lax.broadcasted_iota(jnp.int32, (128, 128), 0) == coarse_map[pl.ds(0, 1), :]
    return jnp.sum(jnp.where(hit, sol, 0.0), axis=0, keepdims=True)


def first_kernel(place, w, c2, ze, zo, xe, xo, basis, eigen, oe, oo, r, z0, z9, x0, x9, zl, zh, xl, xh, xu, xd, *work):
    z_low = place[0] == 0
    x_low = place[1] == 0
    zh[...] = pick(z_low, ze, zo, 0, FACE)
    zl[...] = pick(z_low, zo, ze, 0, FACE)
    xh[...] = jnp.where(place[3] == 1, pick(x_low, xe, xo, 0, FACE), 0.0)
    xl[...] = jnp.where(place[2] == 1, pick(x_low, xo, xe, 0, FACE), 0.0)
    solve(w, zl, zh, xl, xh, basis, eigen, r, z0, z9, x0, x9, *work)
    for message, face, i in ((xu, x9, 7), (xd, x0, 0)):
        message[pl.ds(0, FACE), :] = face[...]
        for k in range(8):
            here = pl.ds(k * 64 + i * 8, 8)
            message[pl.ds(FACE + k * 8, 8), :] = w[here, :] - c2[here, :] * r[here, :]
        message[pl.ds(128, 8), :] = z9[pl.ds(i * 8, 8), :]
        message[pl.ds(136, 8), :] = z0[pl.ds(i * 8, 8), :]
    oe[...] = jnp.where(x_low, xu[...], xd[...])
    oo[pl.ds(0, LINK), :] = jnp.where(x_low, xd[...], xu[...])


def middle_kernel(place, r, w, c2, z0, z9, xe, xo, terms, ze, zo, r2, grouped, zu, zd):
    x_low = place[1] == 0
    above = jnp.where(place[3] == 1, pick(x_low, xe, xo, 0, LINK), 0.0)
    below = jnp.where(place[2] == 1, pick(x_low, xo, xe, 0, LINK), 0.0)
    r2[...] = r[...]
    for k in range(8):
        r2[pl.ds(k * 64 + 56, 8), :] += above[k * 8 : k * 8 + 8]
        r2[pl.ds(k * 64, 8), :] += below[k * 8 : k * 8 + 8]
    for message, face, k, edge in ((zu, z9, 7, 128), (zd, z0, 0, 136)):
        message[pl.ds(0, FACE), :] = face[...]
        message[pl.ds(FACE, FACE), :] = w[layer(k), :] - c2[layer(k), :] * r2[layer(k), :]
        message[pl.ds(128, 8), :] = below[edge : edge + 8]
        message[pl.ds(136, 8), :] = above[edge : edge + 8]
    ze[pl.ds(0, LINK), :] = jnp.where(place[0] == 0, zu[...], zd[...])
    zo[...] = jnp.where(place[0] == 0, zd[...], zu[...])
    grouped[...] = terms[...] + xo[pl.ds(LINK, 8), :]
    ze[pl.ds(LINK, 8), :] = grouped[...]


def second_kernel(
    place, r2, w, c2, z0, z9, x0, x9, aze, azo, axe, axo, xe, xo, ze, zo, basis, eigen,
    co, ce, de, do, first, field, out, zl, zh, xl, xh, s0, s9, t0, t9, *work
):
    z_low = place[0] == 0
    x_low = place[1] == 0
    from_up = lambda start, rows: pick(z_low, ze, zo, start, rows)
    from_down = lambda start, rows: pick(z_low, zo, ze, start, rows)
    first[...] = r2[...]
    first[layer(7), :] += from_up(0, FACE)
    first[layer(0), :] += from_down(0, FACE)
    zh[...] = from_up(FACE, FACE) - pick(z_low, aze, azo, FACE, FACE) * z9[...]
    zl[...] = from_down(FACE, FACE) - pick(z_low, azo, aze, FACE, FACE) * z0[...]
    xh[...] = x9[...]
    xl[...] = x0[...]
    xl[pl.ds(0, 8), :] += from_down(128, 8)
    xl[pl.ds(56, 8), :] += from_up(128, 8)
    xh[pl.ds(0, 8), :] += from_down(136, 8)
    xh[pl.ds(56, 8), :] += from_up(136, 8)
    value = pick(x_low, xe, xo, FACE, FACE) - pick(x_low, axe, axo, FACE, FACE) * xh[...]
    xh[...] = jnp.where(place[3] == 1, value, 0.0)
    value = pick(x_low, xo, xe, FACE, FACE) - pick(x_low, axo, axe, FACE, FACE) * xl[...]
    xl[...] = jnp.where(place[2] == 1, value, 0.0)
    field[...] = w[...] - c2[...] * first[...]
    solve(field, zl, zh, xl, xh, basis, eigen, out, s0, s9, t0, t9, *work)
    first[...] += out[...]
    ce[...] = jnp.where(z_low, s9[...], s0[...])
    co[pl.ds(0, FACE), :] = jnp.where(z_low, s0[...], s9[...])
    hand_out(x_low, t9, t0, de, do)


def last_kernel(place, first, ze, zo, xe, xo, terms, grouped, own_part, coarse_map, own, group, top, out):
    z_low = place[0] == 0
    x_low = place[1] == 0
    total = terms[...] + zo[pl.ds(FACE, 8), :]
    out[...] = first[...] + correct(total, grouped[...], own_part, coarse_map, own, group, top)
    out[layer(7), :] += pick(z_low, ze, zo, 0, FACE)
    out[layer(0), :] += pick(z_low, zo, ze, 0, FACE)
    above = jnp.where(place[3] == 1, pick(x_low, xe, xo, 0, FACE), 0.0)
    below = jnp.where(place[2] == 1, pick(x_low, xo, xe, 0, FACE), 0.0)
    for k in range(8):
        out[pl.ds(k * 64 + 56, 8), :] += above[k * 8 : k * 8 + 8]
        out[pl.ds(k * 64, 8), :] += below[k * 8 : k * 8 + 8]


def move(value, axis, pairs):
    return lax.ppermute(value, axis, pairs)


def body(residual, margin, diag, basis, eigen, coarse_map, own, group, top):
    shape = residual.shape
    residual, margin, diag = (a.reshape(-1, 128) for a in (residual, margin, diag))
    basis, eigen = (a.reshape(-1, 1, 128) for a in (basis, eigen))
    coarse_map = coarse_map.reshape(1, 128)
    own, group, top = (a.reshape(128, -1) for a in (own, group, top))
    dom, coarse = lax.axis_index("dom"), lax.axis_index("coarse")
    doms, coarses = lax.axis_size("dom"), lax.axis_size("coarse")
    place = jnp.stack([dom % 2, coarse % 2, coarse > 0, coarse < coarses - 1]).astype(jnp.int32)
    z_even, z_odd = swap(doms, 1, 0), swap(doms, 1, 1)
    x_even, x_odd = swap(coarses, 1, 0), swap(coarses, 1, 1)
    is_top = jnp.arange(8)[:, None] < 4
    held = [jax.ShapeDtypeStruct(a.shape, a.dtype) for a in (coarse_map, own, group, top)]

    xe, zo, ze, xo, w, c2, terms, own_part, coarse_map, own, group, top = call(
        pre_kernel, [136, 128, 128, 128, 512, 512, 8, 8] + held, (512,) * 3 + (128,) * 4,
        place, residual, margin, diag, coarse_map, own, group, top,
        in_hbm=range(1, 8), scratch=[pltpu.SemaphoreType.DMA((7,))], flops=300000,
    )
    axe = move(xe, "coarse", x_even)
    azo, aze = move(zo, "dom", z_odd), move(ze, "dom", z_even)
    axo = move(xo, "coarse", x_odd)
    terms = terms + axe[128:]
    beside = move(terms, "dom", swap(doms, 4, 0))
    terms = terms + jnp.where(is_top, beside, 0.0)
    beside = move(terms, "coarse", swap(coarses, 4, 0))
    xe, xo, r, z0, z9, x0, x9 = call(
        first_kernel, (LINK, LINK + 8, 512) + (FACE,) * 4, (FACE,) * 4 + (LINK,) * 2 + SOLVE_SCRATCH,
        place, w, c2, aze, azo, axe, axo, basis, eigen,
    )
    terms = terms + beside
    xo = lax.dynamic_update_slice(xo, terms, (LINK, 0))
    xe, xo = move(xe, "coarse", x_even), move(xo, "coarse", x_odd)
    ze, zo, r2, grouped = call(
        middle_kernel, (LINK + 8, LINK, 512, 8), (LINK,) * 2, place, r, w, c2, z0, z9, xe, xo, terms, flops=300000
    )
    zo, ze = move(zo, "dom", z_odd), move(ze, "dom", z_even)
    terms = grouped + ze[LINK:]
    terms = terms + move(terms, "dom", swap(doms, 8, 0))
    beside = move(terms, "dom", swap(doms, 8, 1))
    co, ce, de, do, first = call(
        second_kernel, (FACE + 8, FACE, FACE, FACE, 512), (512, 512) + (FACE,) * 8 + SOLVE_SCRATCH,
        place, r2, w, c2, z0, z9, x0, x9, aze, azo, axe, axo, xe, xo, ze, zo, basis, eigen,
    )
    terms = terms + beside
    co = lax.dynamic_update_slice(co, terms, (FACE, 0))
    zo, ze = move(co, "dom", z_odd), move(ce, "dom", z_even)
    xe, xo = move(de, "coarse", x_even), move(do, "coarse", x_odd)
    (out,) = call(
        last_kernel, (512,), (),
        place, first, ze, zo, xe, xo, terms, grouped, own_part, coarse_map, own, group, top, flops=300000,
    )
    return out.reshape(shape)


def solution(mesh):
    field = P(None, None, None, "dom", "coarse", None)
    factor = P("dom", "coarse", None, None)
    in_specs = (field, field, field, field, P(None, None, "dom", "coarse", None), P("dom", "coarse", None))
    in_specs = in_specs + (factor, factor, factor)
    return jax.shard_map(body, mesh=mesh, in_specs=in_specs, out_specs=field, check_vma=False)
```

```python
import jax
import jax.numpy as jnp
from jax import lax
from jax.experimental import pallas as pl
from jax.experimental.pallas import tpu as pltpu
from jax.sharding import PartitionSpec as P

sum_scale = 0.015625
F32 = jnp.float32
FACE = 64
LINK = 144
RELAY = 32
VMEM = pl.BlockSpec(memory_space=pltpu.VMEM)


def swap(length, stride, odd):
    ring = length // stride
    pairs = []
    for low in range(odd, ring, 2):
        high = (low + 1) % ring
        pairs += [(low, high), (high, low)]
    return [(a * stride + r, b * stride + r) for a, b in pairs for r in range(stride)]


def within(length, group, odd):
    pairs = swap(group, 1, odd)
    return [(base + a, base + b) for base in range(0, length, group) for a, b in pairs]


def call(kernel, outs, scratch_rows, *args, in_hbm=(), scratch=(), flops=2 * 60000 * 128):
    outs = [jax.ShapeDtypeStruct((out, 128), F32) if isinstance(out, int) else out for out in outs]
    specs = [pl.BlockSpec(memory_space=pltpu.SMEM) if a.ndim == 1 else VMEM for a in args]
    args = list(args)
    for at in in_hbm:
        specs[at] = pl.BlockSpec(memory_space=pltpu.HBM)
        args[at] = pltpu.with_memory_space_constraint(args[at], pltpu.HBM)
    return pl.pallas_call(
        kernel,
        out_shape=outs,
        in_specs=specs,
        out_specs=[VMEM] * len(outs),
        scratch_shapes=[pltpu.VMEM((rows, 128), F32) for rows in scratch_rows] + list(scratch),
        compiler_params=pltpu.CompilerParams(vmem_limit_bytes=8 * 1024 * 1024),
        cost_estimate=pl.CostEstimate(flops=flops, bytes_accessed=1000000, transcendentals=0),
    )(*args)


def rows8(start):
    return pl.ds(pl.multiple_of(start, 8), 8)


def every(start, stride):
    return pl.ds(start, 8, stride=stride)


def weigh(basis, direction, inputs, first_in, outs, forward):
    results = []
    for out in outs:
        total = None
        for at, tiles in enumerate(inputs):
            pair = (first_in + at, out) if forward else (out, first_in + at)
            coef = basis[direction * 100 + pair[0] * 10 + pair[1]]
            terms = [coef * tile for tile in tiles]
            total = terms if total is None else [a + b for a, b in zip(total, terms)]
        results.append(total)
    return results


ALL_TEN = range(10)
INNER = range(1, 9)


def forward_own(field, basis, work, ylow, yhigh, plane):
    def y_face_in(face, at, turn):
        lines = [[pltpu.roll(field[every(k * 64 + at, 8), :], turn, 1)] for k in range(8)]
        for k, (value,) in enumerate(weigh(basis, 0, lines, 1, ALL_TEN, True)):
            plane[rows8(k * 8), :] = value
        lines = [[plane[every(i, 8), :], plane[every(64 + i, 8), :]] for i in range(8)]
        for i, (value, rest) in enumerate(weigh(basis, 1, lines, 1, ALL_TEN, True)):
            face[every(i, 10), :] = value
            face[every(80 + i, 10), :] = rest

    y_face_in(ylow, 7, 1)
    y_face_in(yhigh, 0, 127)

    def forward_z(step, carry):
        tiles = [step * 2, step * 2 + 1]
        lines = [[field[rows8(k * 64 + i * 8), :] for i in tiles] for k in range(8)]
        for k, values in enumerate(weigh(basis, 0, lines, 1, ALL_TEN, True)):
            for i, value in zip(tiles, values):
                work[rows8((k * 10 + i + 1) * 8), :] = value
        return carry

    lax.fori_loop(0, 4, forward_z, 0)


def solve(work_in, ylow_in, yhigh_in, z_low, z_high, x_low, x_high, basis, inverse, work, ylow, yhigh):
    def add_z(step, carry):
        tiles = [step * 2, step * 2 + 1]
        low = [z_low[rows8(i * 8), :] for i in tiles]
        high = [z_high[rows8(i * 8), :] for i in tiles]
        for k in ALL_TEN:
            for i, a, b in zip(tiles, low, high):
                rows = rows8((k * 10 + i + 1) * 8)
                work[rows, :] = work_in[rows, :] + basis[k] * a + basis[90 + k] * b
        return carry

    lax.fori_loop(0, 4, add_z, 0)
    lines = [[x_low[rows8(k * 8), :], x_high[rows8(k * 8), :]] for k in range(8)]
    for k, (low, high) in enumerate(weigh(basis, 0, lines, 1, ALL_TEN, True)):
        work[rows8(k * 80), :] = low
        work[rows8(k * 80 + 72), :] = high

    def turn_x(forward):
        def step_x(step, carry):
            ks = [step * 2, step * 2 + 1]
            lines = [[work[rows8(k * 80 + i * 8), :] for k in ks] for i in range(10)]
            for i, values in enumerate(weigh(basis, 1, lines, 0, ALL_TEN, forward)):
                for k, value in zip(ks, values):
                    work[rows8(k * 80 + i * 8), :] = value
            return carry

        lax.fori_loop(0, 5, step_x, 0)

    turn_x(True)

    def step_y(step, carry):
        rows = rows8(step * 8)
        lines = [[ylow_in[rows, :]]] + [[work[every(step * 64 + j, 8), :]] for j in range(8)] + [[yhigh_in[rows, :]]]
        spectral = weigh(basis, 2, lines, 0, ALL_TEN, True)
        spectral = [[value * inverse[rows8(j * 104 + step * 8), :]] for j, (value,) in enumerate(spectral)]
        solved = weigh(basis, 2, spectral, 0, ALL_TEN, False)
        ylow[rows, :] = solved[0][0]
        yhigh[rows, :] = solved[9][0]
        for j in range(8):
            work[every(step * 64 + j, 8), :] = solved[j + 1][0]
        return carry

    lax.fori_loop(0, 13, step_y, 0)
    turn_x(False)


def back_faces(work, basis, z_face, x_face):
    def back_z(step, carry):
        tiles = [step * 2, step * 2 + 1]
        lines = [[work[rows8((k * 10 + i + 1) * 8), :] for i in tiles] for k in range(10)]
        for at, values in enumerate(weigh(basis, 0, lines, 0, (0, 9), False)):
            for i, value in zip(tiles, values):
                z_face[rows8(at * FACE + i * 8), :] = value
        return carry

    lax.fori_loop(0, 4, back_z, 0)
    lines = [[work[rows8(k * 80), :], work[rows8(k * 80 + 72), :]] for k in range(10)]
    for k, (low, high) in enumerate(weigh(basis, 0, lines, 0, INNER, False)):
        x_face[rows8(k * 8), :] = low
        x_face[rows8(FACE + k * 8), :] = high


def back_inner(work, ylow, yhigh, basis, out, plane, plus=None):
    def back_z(step, carry):
        tiles = [step * 2, step * 2 + 1]
        lines = [[work[rows8((k * 10 + i + 1) * 8), :] for i in tiles] for k in range(10)]
        for k, values in enumerate(weigh(basis, 0, lines, 0, INNER, False)):
            for i, value in zip(tiles, values):
                rows = rows8(k * 64 + i * 8)
                out[rows, :] = value if plus is None else value + plus[rows, :]
        return carry

    lax.fori_loop(0, 4, back_z, 0)

    def y_face_out(face, at, turn):
        lines = [[face[every(i, 10), :], face[every(80 + i, 10), :]] for i in range(10)]
        for i, (value, rest) in enumerate(weigh(basis, 1, lines, 0, INNER, False)):
            plane[rows8(i * 16), :] = value
            plane[rows8(i * 16 + 8), :] = rest
        lines = [[plane[every(k, 16), :]] for k in range(10)]
        for k, (value,) in enumerate(weigh(basis, 0, lines, 0, INNER, False)):
            out[every(k * 64 + at, 8), :] += pltpu.roll(value, turn, 1)

    y_face_out(ylow, 7, 127)
    y_face_out(yhigh, 0, 1)


def layer(k):
    return pl.ds(pl.multiple_of(k * 64, 64), 64)


def face(at):
    return pl.ds(pl.multiple_of(at * FACE, FACE), FACE)


def put_x(ref, base, array, i):
    for k in range(8):
        ref[pl.ds(base + k * 8, 8), :] = array[rows8(k * 64 + i * 8), :]


def pick(flag, array, other, start, rows):
    return jnp.where(flag, array[pl.ds(start, rows), :], other[pl.ds(start, rows), :])


def keep(flag, value):
    return jnp.where(flag == 1, value, 0.0)


def first_kernel(
    place, residual_hbm, margin_hbm, diag_hbm, map_hbm, own_hbm, group_hbm, top_hbm,
    zo, ze, xe, xo, w, c2, terms, own_part, coarse_map, own, group, top, residual, margin, diag, sems
):
    sources = (residual_hbm, margin_hbm, diag_hbm, map_hbm, own_hbm, group_hbm, top_hbm)
    targets = (residual, margin, diag, coarse_map, own, group, top)
    copies = [pltpu.make_async_copy(a, b, sems.at[at]) for at, (a, b) in enumerate(zip(sources, targets))]
    for copy in copies:
        copy.start()
    copies[0].wait()
    copies[1].wait()
    w[...] = margin[...] * residual[...]
    copies[2].wait()
    c2[...] = margin[...] * diag[...]
    z_up, x_up = place[0], place[1]
    for base, source in ((0, w), (FACE, c2)):
        zo[pl.ds(base, FACE), :] = source[layer(z_up * 7), :]
        ze[pl.ds(base, FACE), :] = source[layer(7 - z_up * 7), :]
        put_x(xo, base, source, x_up * 7)
        put_x(xe, base, source, 7 - x_up * 7)
    zo[pl.ds(128, 16), :] = jnp.zeros((16, 128), F32)
    total = w[pl.ds(0, 8), :]
    for at in range(8, 512, 8):
        total = total + w[pl.ds(at, 8), :]
    element_sum = jnp.sum(total, axis=0, keepdims=True) * sum_scale
    for copy in copies[3:]:
        copy.wait()
    hit = lax.broadcasted_iota(jnp.int32, (128, 128), 0) == coarse_map[pl.ds(0, 1), :]
    rhs = jnp.sum(jnp.where(hit, element_sum, 0.0), axis=1, keepdims=True)
    own_part[...] = jnp.zeros((8, 128), F32)
    own_part[pl.ds(0, 1), :] = jnp.sum(own[...] * rhs, axis=0, keepdims=True)
    terms[...] = jnp.zeros((8, 128), F32)
    for at in range(4):
        terms[pl.ds(at, 1), :] = jnp.sum(top[:, at * 128 : (at + 1) * 128] * rhs, axis=0, keepdims=True)
    for at in range(2):
        terms[pl.ds(4 + at, 1), :] = jnp.sum(group[:, at * 128 : (at + 1) * 128] * rhs, axis=0, keepdims=True)
    xe[pl.ds(128, 8), :] = terms[...]
    ze[pl.ds(128, 8), :] = terms[...]


def own_kernel(w, basis, eigen, terms, work, ylow, yhigh, inverse, same, plane, zx):
    same[...] = terms[...]
    forward_own(w, basis, work, ylow, yhigh, plane)
    for k in range(10):
        for i in range(10):
            zx[pl.ds(k * 10 + i, 1), :] = eigen[k] + eigen[10 + i]
    for j in range(10):
        inverse[pl.ds(j * 104, 104), :] = 1.0 / (zx[...] + eigen[20 + j])


def pass_kernel(
    place, w, c2, azo, aze, axo, axe, basis, work_in, ylow_in, yhigh_in, inverse,
    zo, ze, xo, xe, r, z_face, x_face, zl, zh, xl, xh, work, ylow, yhigh, plane
):
    z_low, x_low = place[0] == 0, place[1] == 0
    zh[...] = pick(z_low, aze, azo, 0, FACE)
    zl[...] = pick(z_low, azo, aze, 0, FACE)
    xh[...] = keep(place[3], pick(x_low, axe, axo, 0, FACE))
    xl[...] = keep(place[2], pick(x_low, axo, axe, 0, FACE))
    solve(work_in, ylow_in, yhigh_in, zl, zh, xl, xh, basis, inverse, work, ylow, yhigh)
    back_faces(work, basis, z_face, x_face)
    back_inner(work, ylow, yhigh, basis, r, plane)
    for message, up in ((zo, place[0]), (ze, 1 - place[0])):
        here = layer(up * 7)
        message[pl.ds(0, FACE), :] = z_face[face(up), :]
        message[pl.ds(FACE, FACE), :] = w[here, :] - c2[here, :] * r[here, :]
        message[pl.ds(128, 8), :] = x_face[rows8(FACE + up * 56), :]
        message[pl.ds(136, 8), :] = x_face[rows8(up * 56), :]
    zo[pl.ds(LINK, 8), :] = jnp.zeros((8, 128), F32)
    for message, up in ((xo, place[1]), (xe, 1 - place[1])):
        message[pl.ds(0, FACE), :] = x_face[face(up), :]
        for k in range(8):
            here = rows8(k * 64 + up * 56)
            message[pl.ds(FACE + k * 8, 8), :] = w[here, :] - c2[here, :] * r[here, :]


def relay_kernel(place, zo, ze, terms, ro, re, same):
    same[...] = terms[...]
    z_low = place[0] == 0
    for message, up in ((ro, place[1]), (re, 1 - place[1])):
        edge = rows8(136 - up * 8)
        line = rows8(up * 56)
        message[pl.ds(0, 8), :] = jnp.where(z_low, zo[edge, :], ze[edge, :])
        message[pl.ds(8, 8), :] = jnp.where(z_low, ze[edge, :], zo[edge, :])
        message[pl.ds(16, 8), :] = jnp.where(z_low, zo[line, :], ze[line, :])
        message[pl.ds(24, 8), :] = jnp.where(z_low, ze[line, :], zo[line, :])


def second_own_kernel(place, w, c2, r, zo, ze, xo, xe, basis, terms, first, work, ylow, yhigh, same, field, plane):
    same[...] = terms[...]
    z_low, x_low = place[0] == 0, place[1] == 0
    first[...] = r[...]
    first[layer(7), :] += pick(z_low, ze, zo, 0, FACE)
    first[layer(0), :] += pick(z_low, zo, ze, 0, FACE)
    above = keep(place[3], pick(x_low, xe, xo, 0, FACE))
    below = keep(place[2], pick(x_low, xo, xe, 0, FACE))
    for k in range(8):
        first[pl.ds(k * 64 + 56, 8), :] += above[k * 8 : k * 8 + 8]
        first[pl.ds(k * 64, 8), :] += below[k * 8 : k * 8 + 8]
    field[...] = w[...] - c2[...] * first[...]
    forward_own(field, basis, work, ylow, yhigh, plane)


def second_pass_kernel(
    place, azo, aze, axo, axe, z_face, x_face, zo, ze, xo, xe, ro, re, basis, work_in, ylow_in, yhigh_in, inverse,
    co, ce, do, de, work, ylow, yhigh, zl, zh, xl, xh, s_face, t_face
):
    z_low, x_low = place[0] == 0, place[1] == 0
    above = keep(place[3], pick(x_low, re, ro, 0, RELAY))
    below = keep(place[2], pick(x_low, ro, re, 0, RELAY))
    for halo, start, edge in ((zl, 0, 0), (zh, FACE, 8)):
        halo[...] = z_face[pl.ds(start, FACE), :]
        halo[pl.ds(0, 8), :] += below[edge : edge + 8]
        halo[pl.ds(56, 8), :] += above[edge : edge + 8]
    for halo, start, edges in ((xl, 0, below), (xh, FACE, above)):
        halo[...] = x_face[pl.ds(start, FACE), :]
        halo[pl.ds(0, 8), :] += edges[16:24]
        halo[pl.ds(56, 8), :] += edges[24:32]
    zh[...] = pick(z_low, ze, zo, FACE, FACE) - pick(z_low, aze, azo, FACE, FACE) * zh[...]
    zl[...] = pick(z_low, zo, ze, FACE, FACE) - pick(z_low, azo, aze, FACE, FACE) * zl[...]
    xh[...] = keep(place[3], pick(x_low, xe, xo, FACE, FACE) - pick(x_low, axe, axo, FACE, FACE) * xh[...])
    xl[...] = keep(place[2], pick(x_low, xo, xe, FACE, FACE) - pick(x_low, axo, axe, FACE, FACE) * xl[...])
    solve(work_in, ylow_in, yhigh_in, zl, zh, xl, xh, basis, inverse, work, ylow, yhigh)
    back_faces(work, basis, s_face, t_face)
    for message, up in ((co, place[0]), (ce, 1 - place[0])):
        message[pl.ds(0, FACE), :] = s_face[face(up), :]
    for message, up in ((do, place[1]), (de, 1 - place[1])):
        message[...] = t_face[face(up), :]


def inner_kernel(first, work, ylow, yhigh, basis, grouped, own_part, own, group, out, base, plane):
    back_inner(work, ylow, yhigh, basis, out, plane, first)
    sums = own[...] * own_part[pl.ds(0, 1), :]
    for at in range(2):
        sums = sums + group[:, at * 128 : (at + 1) * 128] * grouped[pl.ds(4 + at, 1), :]
    base[...] = sums


def last_kernel(place, inner, base, zo, ze, xo, xe, terms, coarse_map, top, out):
    z_low, x_low = place[0] == 0, place[1] == 0
    total = terms[...] + zo[pl.ds(FACE, 8), :]
    sums = base[...]
    for at in range(4):
        sums = sums + top[:, at * 128 : (at + 1) * 128] * total[at : at + 1]
    sol = jnp.sum(sums, axis=1, keepdims=True)
    hit = lax.broadcasted_iota(jnp.int32, (128, 128), 0) == coarse_map[pl.ds(0, 1), :]
    out[...] = inner[...] + jnp.sum(jnp.where(hit, sol, 0.0), axis=0, keepdims=True)
    out[layer(7), :] += pick(z_low, ze, zo, 0, FACE)
    out[layer(0), :] += pick(z_low, zo, ze, 0, FACE)
    above = keep(place[3], pick(x_low, xe, xo, 0, FACE))
    below = keep(place[2], pick(x_low, xo, xe, 0, FACE))
    for k in range(8):
        out[pl.ds(k * 64 + 56, 8), :] += above[k * 8 : k * 8 + 8]
        out[pl.ds(k * 64, 8), :] += below[k * 8 : k * 8 + 8]


def move(value, axis, pairs):
    return lax.ppermute(value, axis, pairs)


def body(residual, margin, diag, basis, eigen, coarse_map, own, group, top):
    shape = residual.shape
    residual, margin, diag = (a.reshape(-1, 128) for a in (residual, margin, diag))
    basis, eigen = (a.reshape(-1, 1, 128) for a in (basis, eigen))
    coarse_map = coarse_map.reshape(1, 128)
    own, group, top = (a.reshape(128, -1) for a in (own, group, top))
    dom, coarse = lax.axis_index("dom"), lax.axis_index("coarse")
    doms, coarses = lax.axis_size("dom"), lax.axis_size("coarse")
    place = jnp.stack([dom % 2, coarse % 2, coarse > 0, coarse < coarses - 1]).astype(jnp.int32)
    z_even, z_odd = swap(doms, 1, 0), swap(doms, 1, 1)
    x_even, x_odd = swap(coarses, 1, 0), swap(coarses, 1, 1)
    inner_rows = (840, 160, 160)

    both = [(i, i ^ (coarses + 1)) for i in range(doms * coarses)]
    is_top = jnp.arange(8)[:, None] < 4
    held = [jax.ShapeDtypeStruct(a.shape, a.dtype) for a in (coarse_map, own, group, top)]

    zo, ze, xe, xo, w, c2, terms, own_part, coarse_map, own, group, top = call(
        first_kernel, [144, 136, 136, 128, 512, 512, 8, 8] + held, (512,) * 3,
        place, residual, margin, diag, coarse_map, own, group, top,
        in_hbm=range(1, 8), scratch=[pltpu.SemaphoreType.DMA((7,))], flops=300000,
    )
    azo, aze = move(zo, "dom", z_odd), move(ze, "dom", z_even)
    axe, axo = move(xe, "coarse", x_even), move(xo, "coarse", x_odd)
    across = move(terms, ("dom", "coarse"), both)
    work, ylow, yhigh, inverse, terms = call(
        own_kernel, inner_rows + (1040, 8), (128, 104), w, basis, eigen, terms, flops=20000000
    )
    terms = terms + axe[128:] + jnp.where(is_top, aze[128:] + across, 0.0)
    beside = move(terms, "coarse", swap(coarses, 4, 0))
    zo, ze, xo, xe, r, z_face, x_face = call(
        pass_kernel, (LINK + 8, LINK, 136, 128, 512, 128, 128), (FACE,) * 4 + inner_rows + (128,),
        place, w, c2, azo, aze, axo, axe, basis, work, ylow, yhigh, inverse,
    )
    terms = terms + beside
    zo, ze = move(zo, "dom", z_odd), move(ze, "dom", z_even)
    xo = move(lax.dynamic_update_slice(xo, terms, (128, 0)), "coarse", x_odd)
    xe = move(xe, "coarse", x_even)
    grouped = terms + xo[128:]
    terms = grouped + move(grouped, "dom", swap(doms, 4, 0))
    ro, re, terms = call(relay_kernel, (RELAY, RELAY, 8), (), place, zo, ze, terms, flops=1000)
    re, ro = move(re, "coarse", x_even), move(ro, "coarse", x_odd)
    beside = move(terms, "dom", swap(doms, 8, 0))
    first, work, ylow, yhigh, terms = call(
        second_own_kernel, (512,) + inner_rows + (8,), (512, 128), place, w, c2, r, zo, ze, xo, xe, basis, terms, flops=1000
    )
    terms = terms + beside
    beside = move(terms, "dom", swap(doms, 8, 1))
    co, ce, do, de, work, ylow, yhigh = call(
        second_pass_kernel, (FACE + 8, FACE, FACE, FACE) + inner_rows, (FACE,) * 4 + (128,) * 2,
        place, azo, aze, axo, axe, z_face, x_face, zo, ze, xo, xe, ro, re, basis, work, ylow, yhigh, inverse,
    )
    terms = terms + beside
    zo = move(lax.dynamic_update_slice(co, terms, (FACE, 0)), "dom", z_odd)
    ze = move(ce, "dom", z_even)
    xe, xo = move(de, "coarse", x_even), move(do, "coarse", x_odd)
    inner, base = call(
        inner_kernel, (512, 128), (128,), first, work, ylow, yhigh, basis, grouped, own_part, own, group, flops=1000
    )
    (out,) = call(last_kernel, (512,), (), place, inner, base, zo, ze, xo, xe, terms, coarse_map, top, flops=300000)
    return out.reshape(shape)


def solution(mesh):
    field = P(None, None, None, "dom", "coarse", None)
    factor = P("dom", "coarse", None, None)
    in_specs = (field, field, field, field, P(None, None, "dom", "coarse", None), P("dom", "coarse", None))
    in_specs = in_specs + (factor, factor, factor)
    return jax.shard_map(body, mesh=mesh, in_specs=in_specs, out_specs=field, check_vma=False)
```

```python
import jax
import jax.numpy as jnp
from jax import lax
from jax.experimental import pallas as pl
from jax.experimental.pallas import tpu as pltpu
from jax.sharding import PartitionSpec as P

sum_scale = 0.015625
F32 = jnp.float32
FACE = 64
LINK = 144
RELAY = 32
VMEM = pl.BlockSpec(memory_space=pltpu.VMEM)


def where_am_i():
    dom, coarse = lax.axis_index("dom"), lax.axis_index("coarse")
    last = lax.axis_size("coarse") - 1
    return dom % 2, coarse % 2, (coarse > 0).astype(jnp.int32), (coarse < last).astype(jnp.int32)


def swap(length, stride, odd):
    ring = length // stride
    pairs = []
    for low in range(odd, ring, 2):
        high = (low + 1) % ring
        pairs += [(low, high), (high, low)]
    return [(a * stride + r, b * stride + r) for a, b in pairs for r in range(stride)]


def within(length, group, odd):
    pairs = swap(group, 1, odd)
    return [(base + a, base + b) for base in range(0, length, group) for a, b in pairs]


def call(kernel, outs, scratch_rows, *args, in_hbm=(), scratch=(), flops=2 * 60000 * 128):
    outs = [jax.ShapeDtypeStruct((out, 128), F32) if isinstance(out, int) else out for out in outs]
    specs = [VMEM] * len(args)
    args = list(args)
    for at in in_hbm:
        specs[at] = pl.BlockSpec(memory_space=pltpu.HBM)
        args[at] = pltpu.with_memory_space_constraint(args[at], pltpu.HBM)
    return pl.pallas_call(
        kernel,
        out_shape=outs,
        in_specs=specs,
        out_specs=[VMEM] * len(outs),
        scratch_shapes=[pltpu.VMEM((rows, 128), F32) for rows in scratch_rows] + list(scratch),
        compiler_params=pltpu.CompilerParams(vmem_limit_bytes=8 * 1024 * 1024),
        cost_estimate=pl.CostEstimate(flops=flops, bytes_accessed=1000000, transcendentals=0),
    )(*args)


def rows8(start):
    return pl.ds(pl.multiple_of(start, 8), 8)


def every(start, stride):
    return pl.ds(start, 8, stride=stride)


def weigh(basis, direction, inputs, first_in, outs, forward):
    results = []
    for out in outs:
        total = None
        for at, tiles in enumerate(inputs):
            pair = (first_in + at, out) if forward else (out, first_in + at)
            coef = basis[direction * 100 + pair[0] * 10 + pair[1]]
            terms = [coef * tile for tile in tiles]
            total = terms if total is None else [a + b for a, b in zip(total, terms)]
        results.append(total)
    return results


ALL_TEN = range(10)
INNER = range(1, 9)


def forward_own(field, basis, work, ylow, yhigh, plane):
    def y_face_in(face, at, turn):
        lines = [[pltpu.roll(field[every(k * 64 + at, 8), :], turn, 1)] for k in range(8)]
        for k, (value,) in enumerate(weigh(basis, 0, lines, 1, ALL_TEN, True)):
            plane[rows8(k * 8), :] = value
        lines = [[plane[every(i, 8), :], plane[every(64 + i, 8), :]] for i in range(8)]
        for i, (value, rest) in enumerate(weigh(basis, 1, lines, 1, ALL_TEN, True)):
            face[every(i, 10), :] = value
            face[every(80 + i, 10), :] = rest

    y_face_in(ylow, 7, 1)
    y_face_in(yhigh, 0, 127)

    def forward_z(step, carry):
        tiles = [step * 2, step * 2 + 1]
        lines = [[field[rows8(k * 64 + i * 8), :] for i in tiles] for k in range(8)]
        for k, values in enumerate(weigh(basis, 0, lines, 1, ALL_TEN, True)):
            for i, value in zip(tiles, values):
                work[rows8((k * 10 + i + 1) * 8), :] = value
        return carry

    lax.fori_loop(0, 4, forward_z, 0)


def solve(work_in, ylow_in, yhigh_in, z_low, z_high, x_low, x_high, basis, inverse, work, ylow, yhigh):
    def add_z(step, carry):
        tiles = [step * 2, step * 2 + 1]
        low = [z_low[rows8(i * 8), :] for i in tiles]
        high = [z_high[rows8(i * 8), :] for i in tiles]
        for k in ALL_TEN:
            for i, a, b in zip(tiles, low, high):
                rows = rows8((k * 10 + i + 1) * 8)
                work[rows, :] = work_in[rows, :] + basis[k] * a + basis[90 + k] * b
        return carry

    lax.fori_loop(0, 4, add_z, 0)
    lines = [[x_low[rows8(k * 8), :], x_high[rows8(k * 8), :]] for k in range(8)]
    for k, (low, high) in enumerate(weigh(basis, 0, lines, 1, ALL_TEN, True)):
        work[rows8(k * 80), :] = low
        work[rows8(k * 80 + 72), :] = high

    def turn_x(forward):
        def step_x(step, carry):
            ks = [step * 2, step * 2 + 1]
            lines = [[work[rows8(k * 80 + i * 8), :] for k in ks] for i in range(10)]
            for i, values in enumerate(weigh(basis, 1, lines, 0, ALL_TEN, forward)):
                for k, value in zip(ks, values):
                    work[rows8(k * 80 + i * 8), :] = value
            return carry

        lax.fori_loop(0, 5, step_x, 0)

    turn_x(True)

    def step_y(step, carry):
        rows = rows8(step * 8)
        lines = [[ylow_in[rows, :]]] + [[work[every(step * 64 + j, 8), :]] for j in range(8)] + [[yhigh_in[rows, :]]]
        spectral = weigh(basis, 2, lines, 0, ALL_TEN, True)
        spectral = [[value * inverse[rows8(j * 104 + step * 8), :]] for j, (value,) in enumerate(spectral)]
        solved = weigh(basis, 2, spectral, 0, ALL_TEN, False)
        ylow[rows, :] = solved[0][0]
        yhigh[rows, :] = solved[9][0]
        for j in range(8):
            work[every(step * 64 + j, 8), :] = solved[j + 1][0]
        return carry

    lax.fori_loop(0, 13, step_y, 0)
    turn_x(False)


def back_faces(work, basis, z_face, x_face):
    def back_z(step, carry):
        tiles = [step * 2, step * 2 + 1]
        lines = [[work[rows8((k * 10 + i + 1) * 8), :] for i in tiles] for k in range(10)]
        for at, values in enumerate(weigh(basis, 0, lines, 0, (0, 9), False)):
            for i, value in zip(tiles, values):
                z_face[rows8(at * FACE + i * 8), :] = value
        return carry

    lax.fori_loop(0, 4, back_z, 0)
    lines = [[work[rows8(k * 80), :], work[rows8(k * 80 + 72), :]] for k in range(10)]
    for k, (low, high) in enumerate(weigh(basis, 0, lines, 0, INNER, False)):
        x_face[rows8(k * 8), :] = low
        x_face[rows8(FACE + k * 8), :] = high


def back_inner(work, ylow, yhigh, basis, out, plane, plus=None):
    def back_z(step, carry):
        tiles = [step * 2, step * 2 + 1]
        lines = [[work[rows8((k * 10 + i + 1) * 8), :] for i in tiles] for k in range(10)]
        for k, values in enumerate(weigh(basis, 0, lines, 0, INNER, False)):
            for i, value in zip(tiles, values):
                rows = rows8(k * 64 + i * 8)
                out[rows, :] = value if plus is None else value + plus[rows, :]
        return carry

    lax.fori_loop(0, 4, back_z, 0)

    def y_face_out(face, at, turn):
        lines = [[face[every(i, 10), :], face[every(80 + i, 10), :]] for i in range(10)]
        for i, (value, rest) in enumerate(weigh(basis, 1, lines, 0, INNER, False)):
            plane[rows8(i * 16), :] = value
            plane[rows8(i * 16 + 8), :] = rest
        lines = [[plane[every(k, 16), :]] for k in range(10)]
        for k, (value,) in enumerate(weigh(basis, 0, lines, 0, INNER, False)):
            out[every(k * 64 + at, 8), :] += pltpu.roll(value, turn, 1)

    y_face_out(ylow, 7, 127)
    y_face_out(yhigh, 0, 1)


def layer(k):
    return pl.ds(pl.multiple_of(k * 64, 64), 64)


def face(at):
    return pl.ds(pl.multiple_of(at * FACE, FACE), FACE)


def put_x(ref, base, array, i):
    for k in range(8):
        ref[pl.ds(base + k * 8, 8), :] = array[rows8(k * 64 + i * 8), :]


def pick(flag, array, other, start, rows):
    return jnp.where(flag, array[pl.ds(start, rows), :], other[pl.ds(start, rows), :])


def keep(flag, value):
    return jnp.where(flag == 1, value, 0.0)


def first_kernel(
    residual_hbm, margin_hbm, diag_hbm, map_hbm, own_hbm, group_hbm, top_hbm,
    zo, ze, xe, xo, w, c2, terms, own_part, coarse_map, own, group, top, residual, margin, diag, sems
):
    place = where_am_i()
    sources = (residual_hbm, margin_hbm, diag_hbm, map_hbm, own_hbm, group_hbm, top_hbm)
    targets = (residual, margin, diag, coarse_map, own, group, top)
    copies = [pltpu.make_async_copy(a, b, sems.at[at]) for at, (a, b) in enumerate(zip(sources, targets))]
    for copy in copies:
        copy.start()
    copies[0].wait()
    copies[1].wait()
    w[...] = margin[...] * residual[...]
    copies[2].wait()
    c2[...] = margin[...] * diag[...]
    z_up, x_up = place[0], place[1]
    for base, source in ((0, w), (FACE, c2)):
        zo[pl.ds(base, FACE), :] = source[layer(z_up * 7), :]
        ze[pl.ds(base, FACE), :] = source[layer(7 - z_up * 7), :]
        put_x(xo, base, source, x_up * 7)
        put_x(xe, base, source, 7 - x_up * 7)
    zo[pl.ds(128, 16), :] = jnp.zeros((16, 128), F32)
    total = w[pl.ds(0, 8), :]
    for at in range(8, 512, 8):
        total = total + w[pl.ds(at, 8), :]
    element_sum = jnp.sum(total, axis=0, keepdims=True) * sum_scale
    for copy in copies[3:]:
        copy.wait()
    hit = lax.broadcasted_iota(jnp.int32, (128, 128), 0) == coarse_map[pl.ds(0, 1), :]
    rhs = jnp.sum(jnp.where(hit, element_sum, 0.0), axis=1, keepdims=True)
    own_part[...] = jnp.zeros((8, 128), F32)
    own_part[pl.ds(0, 1), :] = jnp.sum(own[...] * rhs, axis=0, keepdims=True)
    terms[...] = jnp.zeros((8, 128), F32)
    for at in range(4):
        terms[pl.ds(at, 1), :] = jnp.sum(top[:, at * 128 : (at + 1) * 128] * rhs, axis=0, keepdims=True)
    for at in range(2):
        terms[pl.ds(4 + at, 1), :] = jnp.sum(group[:, at * 128 : (at + 1) * 128] * rhs, axis=0, keepdims=True)
    xe[pl.ds(128, 8), :] = terms[...]
    ze[pl.ds(128, 8), :] = terms[...]


def own_kernel(w, basis, eigen, terms, work, ylow, yhigh, inverse, same, plane, zx):
    same[...] = terms[...]
    forward_own(w, basis, work, ylow, yhigh, plane)
    for k in range(10):
        for i in range(10):
            zx[pl.ds(k * 10 + i, 1), :] = eigen[k] + eigen[10 + i]
    for j in range(10):
        inverse[pl.ds(j * 104, 104), :] = 1.0 / (zx[...] + eigen[20 + j])


def pass_kernel(
    w, c2, azo, aze, axo, axe, basis, work_in, ylow_in, yhigh_in, inverse,
    zo, ze, xo, xe, r, z_face, x_face, zl, zh, xl, xh, work, ylow, yhigh, plane
):
    place = where_am_i()
    z_low, x_low = place[0] == 0, place[1] == 0
    zh[...] = pick(z_low, aze, azo, 0, FACE)
    zl[...] = pick(z_low, azo, aze, 0, FACE)
    xh[...] = keep(place[3], pick(x_low, axe, axo, 0, FACE))
    xl[...] = keep(place[2], pick(x_low, axo, axe, 0, FACE))
    solve(work_in, ylow_in, yhigh_in, zl, zh, xl, xh, basis, inverse, work, ylow, yhigh)
    back_faces(work, basis, z_face, x_face)
    back_inner(work, ylow, yhigh, basis, r, plane)
    for message, up in ((zo, place[0]), (ze, 1 - place[0])):
        here = layer(up * 7)
        message[pl.ds(0, FACE), :] = z_face[face(up), :]
        message[pl.ds(FACE, FACE), :] = w[here, :] - c2[here, :] * r[here, :]
        message[pl.ds(128, 8), :] = x_face[rows8(FACE + up * 56), :]
        message[pl.ds(136, 8), :] = x_face[rows8(up * 56), :]
    zo[pl.ds(LINK, 8), :] = jnp.zeros((8, 128), F32)
    for message, up in ((xo, place[1]), (xe, 1 - place[1])):
        message[pl.ds(0, FACE), :] = x_face[face(up), :]
        for k in range(8):
            here = rows8(k * 64 + up * 56)
            message[pl.ds(FACE + k * 8, 8), :] = w[here, :] - c2[here, :] * r[here, :]


def relay_kernel(zo, ze, terms, ro, re, same):
    place = where_am_i()
    same[...] = terms[...]
    z_low = place[0] == 0
    for message, up in ((ro, place[1]), (re, 1 - place[1])):
        edge = rows8(136 - up * 8)
        line = rows8(up * 56)
        message[pl.ds(0, 8), :] = jnp.where(z_low, zo[edge, :], ze[edge, :])
        message[pl.ds(8, 8), :] = jnp.where(z_low, ze[edge, :], zo[edge, :])
        message[pl.ds(16, 8), :] = jnp.where(z_low, zo[line, :], ze[line, :])
        message[pl.ds(24, 8), :] = jnp.where(z_low, ze[line, :], zo[line, :])


def second_own_kernel(w, c2, r, zo, ze, xo, xe, basis, terms, first, work, ylow, yhigh, same, field, plane):
    place = where_am_i()
    same[...] = terms[...]
    z_low, x_low = place[0] == 0, place[1] == 0
    first[...] = r[...]
    first[layer(7), :] += pick(z_low, ze, zo, 0, FACE)
    first[layer(0), :] += pick(z_low, zo, ze, 0, FACE)
    above = keep(place[3], pick(x_low, xe, xo, 0, FACE))
    below = keep(place[2], pick(x_low, xo, xe, 0, FACE))
    for k in range(8):
        first[pl.ds(k * 64 + 56, 8), :] += above[k * 8 : k * 8 + 8]
        first[pl.ds(k * 64, 8), :] += below[k * 8 : k * 8 + 8]
    field[...] = w[...] - c2[...] * first[...]
    forward_own(field, basis, work, ylow, yhigh, plane)


def second_pass_kernel(
    azo, aze, axo, axe, z_face, x_face, zo, ze, xo, xe, ro, re, basis, work_in, ylow_in, yhigh_in, inverse,
    co, ce, do, de, work, ylow, yhigh, zl, zh, xl, xh, s_face, t_face
):
    place = where_am_i()
    z_low, x_low = place[0] == 0, place[1] == 0
    above = keep(place[3], pick(x_low, re, ro, 0, RELAY))
    below = keep(place[2], pick(x_low, ro, re, 0, RELAY))
    for halo, start, edge in ((zl, 0, 0), (zh, FACE, 8)):
        halo[...] = z_face[pl.ds(start, FACE), :]
        halo[pl.ds(0, 8), :] += below[edge : edge + 8]
        halo[pl.ds(56, 8), :] += above[edge : edge + 8]
    for halo, start, edges in ((xl, 0, below), (xh, FACE, above)):
        halo[...] = x_face[pl.ds(start, FACE), :]
        halo[pl.ds(0, 8), :] += edges[16:24]
        halo[pl.ds(56, 8), :] += edges[24:32]
    zh[...] = pick(z_low, ze, zo, FACE, FACE) - pick(z_low, aze, azo, FACE, FACE) * zh[...]
    zl[...] = pick(z_low, zo, ze, FACE, FACE) - pick(z_low, azo, aze, FACE, FACE) * zl[...]
    xh[...] = keep(place[3], pick(x_low, xe, xo, FACE, FACE) - pick(x_low, axe, axo, FACE, FACE) * xh[...])
    xl[...] = keep(place[2], pick(x_low, xo, xe, FACE, FACE) - pick(x_low, axo, axe, FACE, FACE) * xl[...])
    solve(work_in, ylow_in, yhigh_in, zl, zh, xl, xh, basis, inverse, work, ylow, yhigh)
    back_faces(work, basis, s_face, t_face)
    for message, up in ((co, place[0]), (ce, 1 - place[0])):
        message[pl.ds(0, FACE), :] = s_face[face(up), :]
    for message, up in ((do, place[1]), (de, 1 - place[1])):
        message[...] = t_face[face(up), :]


def inner_kernel(first, work, ylow, yhigh, basis, grouped, own_part, own, group, out, base, plane):
    back_inner(work, ylow, yhigh, basis, out, plane, first)
    sums = own[...] * own_part[pl.ds(0, 1), :]
    for at in range(2):
        sums = sums + group[:, at * 128 : (at + 1) * 128] * grouped[pl.ds(4 + at, 1), :]
    base[...] = sums


def last_kernel(inner, base, zo, ze, xo, xe, terms, coarse_map, top, out):
    place = where_am_i()
    z_low, x_low = place[0] == 0, place[1] == 0
    total = terms[...] + zo[pl.ds(FACE, 8), :]
    sums = base[...]
    for at in range(4):
        sums = sums + top[:, at * 128 : (at + 1) * 128] * total[at : at + 1]
    sol = jnp.sum(sums, axis=1, keepdims=True)
    hit = lax.broadcasted_iota(jnp.int32, (128, 128), 0) == coarse_map[pl.ds(0, 1), :]
    out[...] = inner[...] + jnp.sum(jnp.where(hit, sol, 0.0), axis=0, keepdims=True)
    out[layer(7), :] += pick(z_low, ze, zo, 0, FACE)
    out[layer(0), :] += pick(z_low, zo, ze, 0, FACE)
    above = keep(place[3], pick(x_low, xe, xo, 0, FACE))
    below = keep(place[2], pick(x_low, xo, xe, 0, FACE))
    for k in range(8):
        out[pl.ds(k * 64 + 56, 8), :] += above[k * 8 : k * 8 + 8]
        out[pl.ds(k * 64, 8), :] += below[k * 8 : k * 8 + 8]


def move(value, axis, pairs):
    return lax.ppermute(value, axis, pairs)


def body(residual, margin, diag, basis, eigen, coarse_map, own, group, top):
    shape = residual.shape
    residual, margin, diag = (a.reshape(-1, 128) for a in (residual, margin, diag))
    basis, eigen = (a.reshape(-1, 1, 128) for a in (basis, eigen))
    coarse_map = coarse_map.reshape(1, 128)
    own, group, top = (a.reshape(128, -1) for a in (own, group, top))
    doms, coarses = lax.axis_size("dom"), lax.axis_size("coarse")
    z_even, z_odd = swap(doms, 1, 0), swap(doms, 1, 1)
    x_even, x_odd = swap(coarses, 1, 0), swap(coarses, 1, 1)
    inner_rows = (840, 160, 160)

    both = [(i, i ^ (coarses + 1)) for i in range(doms * coarses)]
    is_top = jnp.arange(8)[:, None] < 4
    held = [jax.ShapeDtypeStruct(a.shape, a.dtype) for a in (coarse_map, own, group, top)]

    zo, ze, xe, xo, w, c2, terms, own_part, coarse_map, own, group, top = call(
        first_kernel, [144, 136, 136, 128, 512, 512, 8, 8] + held, (512,) * 3,
        residual, margin, diag, coarse_map, own, group, top,
        in_hbm=range(7), scratch=[pltpu.SemaphoreType.DMA((7,))], flops=300000,
    )
    azo, aze = move(zo, "dom", z_odd), move(ze, "dom", z_even)
    axe, axo = move(xe, "coarse", x_even), move(xo, "coarse", x_odd)
    across = move(terms, ("dom", "coarse"), both)
    work, ylow, yhigh, inverse, terms = call(
        own_kernel, inner_rows + (1040, 8), (128, 104), w, basis, eigen, terms, flops=20000000
    )
    terms = terms + axe[128:] + jnp.where(is_top, aze[128:] + across, 0.0)
    beside = move(terms, "coarse", swap(coarses, 4, 0))
    zo, ze, xo, xe, r, z_face, x_face = call(
        pass_kernel, (LINK + 8, LINK, 136, 128, 512, 128, 128), (FACE,) * 4 + inner_rows + (128,),
        w, c2, azo, aze, axo, axe, basis, work, ylow, yhigh, inverse,
    )
    terms = terms + beside
    zo, ze = move(zo, "dom", z_odd), move(ze, "dom", z_even)
    xo = move(lax.dynamic_update_slice(xo, terms, (128, 0)), "coarse", x_odd)
    xe = move(xe, "coarse", x_even)
    grouped = terms + xo[128:]
    terms = grouped + move(grouped, "dom", swap(doms, 4, 0))
    ro, re, terms = call(relay_kernel, (RELAY, RELAY, 8), (), zo, ze, terms, flops=1000)
    re, ro = move(re, "coarse", x_even), move(ro, "coarse", x_odd)
    beside = move(terms, "dom", swap(doms, 8, 0))
    first, work, ylow, yhigh, terms = call(
        second_own_kernel, (512,) + inner_rows + (8,), (512, 128), w, c2, r, zo, ze, xo, xe, basis, terms, flops=1000
    )
    terms = terms + beside
    beside = move(terms, "dom", swap(doms, 8, 1))
    co, ce, do, de, work, ylow, yhigh = call(
        second_pass_kernel, (FACE + 8, FACE, FACE, FACE) + inner_rows, (FACE,) * 4 + (128,) * 2,
        azo, aze, axo, axe, z_face, x_face, zo, ze, xo, xe, ro, re, basis, work, ylow, yhigh, inverse,
    )
    terms = terms + beside
    zo = move(lax.dynamic_update_slice(co, terms, (FACE, 0)), "dom", z_odd)
    ze = move(ce, "dom", z_even)
    xe, xo = move(de, "coarse", x_even), move(do, "coarse", x_odd)
    inner, base = call(
        inner_kernel, (512, 128), (128,), first, work, ylow, yhigh, basis, grouped, own_part, own, group, flops=1000
    )
    (out,) = call(last_kernel, (512,), (), inner, base, zo, ze, xo, xe, terms, coarse_map, top, flops=300000)
    return out.reshape(shape)


def solution(mesh):
    field = P(None, None, None, "dom", "coarse", None)
    factor = P("dom", "coarse", None, None)
    in_specs = (field, field, field, field, P(None, None, "dom", "coarse", None), P("dom", "coarse", None))
    in_specs = in_specs + (factor, factor, factor)
    return jax.shard_map(body, mesh=mesh, in_specs=in_specs, out_specs=field, check_vma=False)
```

```python
import jax
import jax.numpy as jnp
from jax import lax
from jax.experimental import pallas as pl
from jax.experimental.pallas import tpu as pltpu
from jax.sharding import PartitionSpec as P

sum_scale = 0.015625
F32 = jnp.float32
FACE = 64
LINK = 144
RELAY = 32
VMEM = pl.BlockSpec(memory_space=pltpu.VMEM)


def where_am_i():
    dom, coarse = lax.axis_index("dom"), lax.axis_index("coarse")
    last = lax.axis_size("coarse") - 1
    return dom % 2, coarse % 2, (coarse > 0).astype(jnp.int32), (coarse < last).astype(jnp.int32)


def swap(length, stride, odd):
    ring = length // stride
    pairs = []
    for low in range(odd, ring, 2):
        high = (low + 1) % ring
        pairs += [(low, high), (high, low)]
    return [(a * stride + r, b * stride + r) for a, b in pairs for r in range(stride)]


def within(length, group, odd):
    pairs = swap(group, 1, odd)
    return [(base + a, base + b) for base in range(0, length, group) for a, b in pairs]


def call(kernel, outs, scratch_rows, *args, in_hbm=(), scratch=(), flops=2 * 60000 * 128):
    outs = [jax.ShapeDtypeStruct((out, 128), F32) if isinstance(out, int) else out for out in outs]
    specs = [VMEM] * len(args)
    args = list(args)
    for at in in_hbm:
        specs[at] = pl.BlockSpec(memory_space=pltpu.HBM)
        args[at] = pltpu.with_memory_space_constraint(args[at], pltpu.HBM)
    return pl.pallas_call(
        kernel,
        out_shape=outs,
        in_specs=specs,
        out_specs=[VMEM] * len(outs),
        scratch_shapes=[pltpu.VMEM((rows, 128), F32) for rows in scratch_rows] + list(scratch),
        compiler_params=pltpu.CompilerParams(vmem_limit_bytes=8 * 1024 * 1024),
        cost_estimate=pl.CostEstimate(flops=flops, bytes_accessed=1000000, transcendentals=0),
    )(*args)


def rows8(start):
    return pl.ds(pl.multiple_of(start, 8), 8)


def every(start, stride):
    return pl.ds(start, 8, stride=stride)


def weigh(basis, direction, inputs, first_in, outs, forward):
    results = []
    for out in outs:
        total = None
        for at, tiles in enumerate(inputs):
            pair = (first_in + at, out) if forward else (out, first_in + at)
            coef = basis[direction * 100 + pair[0] * 10 + pair[1]]
            terms = [coef * tile for tile in tiles]
            total = terms if total is None else [a + b for a, b in zip(total, terms)]
        results.append(total)
    return results


ALL_TEN = range(10)
INNER = range(1, 9)


def forward_own(field, basis, work, ylow, yhigh, plane):
    def y_face_in(face, at, turn):
        lines = [[pltpu.roll(field[every(k * 64 + at, 8), :], turn, 1)] for k in range(8)]
        for k, (value,) in enumerate(weigh(basis, 0, lines, 1, ALL_TEN, True)):
            plane[rows8(k * 8), :] = value
        lines = [[plane[every(i, 8), :], plane[every(64 + i, 8), :]] for i in range(8)]
        for i, (value, rest) in enumerate(weigh(basis, 1, lines, 1, ALL_TEN, True)):
            face[every(i, 10), :] = value
            face[every(80 + i, 10), :] = rest

    y_face_in(ylow, 7, 1)
    y_face_in(yhigh, 0, 127)

    def forward_z(step, carry):
        tiles = [step * 2, step * 2 + 1]
        lines = [[field[rows8(k * 64 + i * 8), :] for i in tiles] for k in range(8)]
        for k, values in enumerate(weigh(basis, 0, lines, 1, ALL_TEN, True)):
            for i, value in zip(tiles, values):
                work[rows8((k * 10 + i + 1) * 8), :] = value
        return carry

    lax.fori_loop(0, 4, forward_z, 0)


def solve(work_in, ylow_in, yhigh_in, z_low, z_high, x_low, x_high, basis, inverse, work, ylow, yhigh):
    def add_z(step, carry):
        tiles = [step * 2, step * 2 + 1]
        low = [z_low[rows8(i * 8), :] for i in tiles]
        high = [z_high[rows8(i * 8), :] for i in tiles]
        for k in ALL_TEN:
            for i, a, b in zip(tiles, low, high):
                rows = rows8((k * 10 + i + 1) * 8)
                work[rows, :] = work_in[rows, :] + basis[k] * a + basis[90 + k] * b
        return carry

    lax.fori_loop(0, 4, add_z, 0)
    lines = [[x_low[rows8(k * 8), :], x_high[rows8(k * 8), :]] for k in range(8)]
    for k, (low, high) in enumerate(weigh(basis, 0, lines, 1, ALL_TEN, True)):
        work[rows8(k * 80), :] = low
        work[rows8(k * 80 + 72), :] = high

    def turn_x(forward):
        def step_x(step, carry):
            ks = [step * 2, step * 2 + 1]
            lines = [[work[rows8(k * 80 + i * 8), :] for k in ks] for i in range(10)]
            for i, values in enumerate(weigh(basis, 1, lines, 0, ALL_TEN, forward)):
                for k, value in zip(ks, values):
                    work[rows8(k * 80 + i * 8), :] = value
            return carry

        lax.fori_loop(0, 5, step_x, 0)

    turn_x(True)

    def step_y(step, carry):
        rows = rows8(step * 8)
        lines = [[ylow_in[rows, :]]] + [[work[every(step * 64 + j, 8), :]] for j in range(8)] + [[yhigh_in[rows, :]]]
        spectral = weigh(basis, 2, lines, 0, ALL_TEN, True)
        spectral = [[value * inverse[rows8(j * 104 + step * 8), :]] for j, (value,) in enumerate(spectral)]
        solved = weigh(basis, 2, spectral, 0, ALL_TEN, False)
        ylow[rows, :] = solved[0][0]
        yhigh[rows, :] = solved[9][0]
        for j in range(8):
            work[every(step * 64 + j, 8), :] = solved[j + 1][0]
        return carry

    lax.fori_loop(0, 13, step_y, 0)
    turn_x(False)


def back_faces(work, basis, z_face, x_face):
    def back_z(step, carry):
        tiles = [step * 2, step * 2 + 1]
        lines = [[work[rows8((k * 10 + i + 1) * 8), :] for i in tiles] for k in range(10)]
        for at, values in enumerate(weigh(basis, 0, lines, 0, (0, 9), False)):
            for i, value in zip(tiles, values):
                z_face[rows8(at * FACE + i * 8), :] = value
        return carry

    lax.fori_loop(0, 4, back_z, 0)
    lines = [[work[rows8(k * 80), :], work[rows8(k * 80 + 72), :]] for k in range(10)]
    for k, (low, high) in enumerate(weigh(basis, 0, lines, 0, INNER, False)):
        x_face[rows8(k * 8), :] = low
        x_face[rows8(FACE + k * 8), :] = high


def back_inner(work, ylow, yhigh, basis, out, plane, plus=None):
    def back_z(step, carry):
        tiles = [step * 2, step * 2 + 1]
        lines = [[work[rows8((k * 10 + i + 1) * 8), :] for i in tiles] for k in range(10)]
        for k, values in enumerate(weigh(basis, 0, lines, 0, INNER, False)):
            for i, value in zip(tiles, values):
                rows = rows8(k * 64 + i * 8)
                out[rows, :] = value if plus is None else value + plus[rows, :]
        return carry

    lax.fori_loop(0, 4, back_z, 0)

    def y_face_out(face, at, turn):
        lines = [[face[every(i, 10), :], face[every(80 + i, 10), :]] for i in range(10)]
        for i, (value, rest) in enumerate(weigh(basis, 1, lines, 0, INNER, False)):
            plane[rows8(i * 16), :] = value
            plane[rows8(i * 16 + 8), :] = rest
        lines = [[plane[every(k, 16), :]] for k in range(10)]
        for k, (value,) in enumerate(weigh(basis, 0, lines, 0, INNER, False)):
            out[every(k * 64 + at, 8), :] += pltpu.roll(value, turn, 1)

    y_face_out(ylow, 7, 127)
    y_face_out(yhigh, 0, 1)


def layer(k):
    return pl.ds(pl.multiple_of(k * 64, 64), 64)


def face(at):
    return pl.ds(pl.multiple_of(at * FACE, FACE), FACE)


def put_x(ref, base, array, i):
    for k in range(8):
        ref[pl.ds(base + k * 8, 8), :] = array[rows8(k * 64 + i * 8), :]


def pick(flag, array, other, start, rows):
    return jnp.where(flag, array[pl.ds(start, rows), :], other[pl.ds(start, rows), :])


def keep(flag, value):
    return jnp.where(flag == 1, value, 0.0)


def first_kernel(
    residual_hbm, margin_hbm, diag_hbm, map_hbm, own_hbm, group_hbm, top_hbm,
    zo, ze, xe, xo, w, c2, terms, own_part, coarse_map, own, group, top, residual, margin, diag, sems
):
    place = where_am_i()
    sources = (residual_hbm, margin_hbm, diag_hbm, map_hbm, own_hbm, group_hbm, top_hbm)
    targets = (residual, margin, diag, coarse_map, own, group, top)
    copies = [pltpu.make_async_copy(a, b, sems.at[at]) for at, (a, b) in enumerate(zip(sources, targets))]
    for copy in copies:
        copy.start()
    copies[0].wait()
    copies[1].wait()
    w[...] = margin[...] * residual[...]
    copies[2].wait()
    c2[...] = margin[...] * diag[...]
    z_up, x_up = place[0], place[1]
    for base, source in ((0, w), (FACE, c2)):
        zo[pl.ds(base, FACE), :] = source[layer(z_up * 7), :]
        ze[pl.ds(base, FACE), :] = source[layer(7 - z_up * 7), :]
        put_x(xo, base, source, x_up * 7)
        put_x(xe, base, source, 7 - x_up * 7)
    total = w[pl.ds(0, 8), :]
    for at in range(8, 512, 8):
        total = total + w[pl.ds(at, 8), :]
    element_sum = jnp.sum(total, axis=0, keepdims=True) * sum_scale
    for copy in copies[3:]:
        copy.wait()
    hit = lax.broadcasted_iota(jnp.int32, (128, 128), 0) == coarse_map[pl.ds(0, 1), :]
    rhs = jnp.sum(jnp.where(hit, element_sum, 0.0), axis=1, keepdims=True)
    own_part[...] = jnp.zeros((8, 128), F32)
    own_part[pl.ds(0, 1), :] = jnp.sum(own[...] * rhs, axis=0, keepdims=True)
    terms[...] = jnp.zeros((8, 128), F32)
    for at in range(4):
        terms[pl.ds(at, 1), :] = jnp.sum(top[:, at * 128 : (at + 1) * 128] * rhs, axis=0, keepdims=True)
    for at in range(2):
        terms[pl.ds(4 + at, 1), :] = jnp.sum(group[:, at * 128 : (at + 1) * 128] * rhs, axis=0, keepdims=True)
    ze[pl.ds(128, 8), :] = terms[...]
    xe[pl.ds(128, 8), :] = terms[...]


def own_kernel(w, basis, eigen, terms, work, ylow, yhigh, inverse, same, plane, zx):
    same[...] = terms[...]
    forward_own(w, basis, work, ylow, yhigh, plane)
    for k in range(10):
        for i in range(10):
            zx[pl.ds(k * 10 + i, 1), :] = eigen[k] + eigen[10 + i]
    for j in range(10):
        inverse[pl.ds(j * 104, 104), :] = 1.0 / (zx[...] + eigen[20 + j])


def pass_kernel(
    w, c2, azo, aze, axo, axe, basis, work_in, ylow_in, yhigh_in, inverse,
    zo, ze, xo, xe, r, z_face, x_face, zl, zh, xl, xh, work, ylow, yhigh, plane
):
    place = where_am_i()
    z_low, x_low = place[0] == 0, place[1] == 0
    zh[...] = pick(z_low, aze, azo, 0, FACE)
    zl[...] = pick(z_low, azo, aze, 0, FACE)
    xh[...] = keep(place[3], pick(x_low, axe, axo, 0, FACE))
    xl[...] = keep(place[2], pick(x_low, axo, axe, 0, FACE))
    solve(work_in, ylow_in, yhigh_in, zl, zh, xl, xh, basis, inverse, work, ylow, yhigh)
    back_faces(work, basis, z_face, x_face)
    back_inner(work, ylow, yhigh, basis, r, plane)
    for message, up in ((zo, place[0]), (ze, 1 - place[0])):
        here = layer(up * 7)
        message[pl.ds(0, FACE), :] = z_face[face(up), :]
        message[pl.ds(FACE, FACE), :] = w[here, :] - c2[here, :] * r[here, :]
        message[pl.ds(128, 8), :] = x_face[rows8(FACE + up * 56), :]
        message[pl.ds(136, 8), :] = x_face[rows8(up * 56), :]
    for message, up in ((xo, place[1]), (xe, 1 - place[1])):
        message[pl.ds(0, FACE), :] = x_face[face(up), :]
        for k in range(8):
            here = rows8(k * 64 + up * 56)
            message[pl.ds(FACE + k * 8, 8), :] = w[here, :] - c2[here, :] * r[here, :]


def relay_kernel(zo, ze, ro, re):
    place = where_am_i()
    z_low = place[0] == 0
    for message, up in ((ro, place[1]), (re, 1 - place[1])):
        edge = rows8(136 - up * 8)
        line = rows8(up * 56)
        message[pl.ds(0, 8), :] = jnp.where(z_low, zo[edge, :], ze[edge, :])
        message[pl.ds(8, 8), :] = jnp.where(z_low, ze[edge, :], zo[edge, :])
        message[pl.ds(16, 8), :] = jnp.where(z_low, zo[line, :], ze[line, :])
        message[pl.ds(24, 8), :] = jnp.where(z_low, ze[line, :], zo[line, :])


def second_own_kernel(w, c2, r, zo, ze, xo, xe, basis, first, work, ylow, yhigh, field, plane):
    place = where_am_i()
    z_low, x_low = place[0] == 0, place[1] == 0
    first[...] = r[...]
    first[layer(7), :] += pick(z_low, ze, zo, 0, FACE)
    first[layer(0), :] += pick(z_low, zo, ze, 0, FACE)
    above = keep(place[3], pick(x_low, xe, xo, 0, FACE))
    below = keep(place[2], pick(x_low, xo, xe, 0, FACE))
    for k in range(8):
        first[pl.ds(k * 64 + 56, 8), :] += above[k * 8 : k * 8 + 8]
        first[pl.ds(k * 64, 8), :] += below[k * 8 : k * 8 + 8]
    field[...] = w[...] - c2[...] * first[...]
    forward_own(field, basis, work, ylow, yhigh, plane)


def second_pass_kernel(
    azo, aze, axo, axe, z_face, x_face, zo, ze, xo, xe, ro, re, basis, work_in, ylow_in, yhigh_in, inverse,
    co, ce, do, de, work, ylow, yhigh, zl, zh, xl, xh, s_face, t_face
):
    place = where_am_i()
    z_low, x_low = place[0] == 0, place[1] == 0
    above = keep(place[3], pick(x_low, re, ro, 0, RELAY))
    below = keep(place[2], pick(x_low, ro, re, 0, RELAY))
    for halo, start, edge in ((zl, 0, 0), (zh, FACE, 8)):
        halo[...] = z_face[pl.ds(start, FACE), :]
        halo[pl.ds(0, 8), :] += below[edge : edge + 8]
        halo[pl.ds(56, 8), :] += above[edge : edge + 8]
    for halo, start, edges in ((xl, 0, below), (xh, FACE, above)):
        halo[...] = x_face[pl.ds(start, FACE), :]
        halo[pl.ds(0, 8), :] += edges[16:24]
        halo[pl.ds(56, 8), :] += edges[24:32]
    zh[...] = pick(z_low, ze, zo, FACE, FACE) - pick(z_low, aze, azo, FACE, FACE) * zh[...]
    zl[...] = pick(z_low, zo, ze, FACE, FACE) - pick(z_low, azo, aze, FACE, FACE) * zl[...]
    xh[...] = keep(place[3], pick(x_low, xe, xo, FACE, FACE) - pick(x_low, axe, axo, FACE, FACE) * xh[...])
    xl[...] = keep(place[2], pick(x_low, xo, xe, FACE, FACE) - pick(x_low, axo, axe, FACE, FACE) * xl[...])
    solve(work_in, ylow_in, yhigh_in, zl, zh, xl, xh, basis, inverse, work, ylow, yhigh)
    back_faces(work, basis, s_face, t_face)
    for message, up in ((co, place[0]), (ce, 1 - place[0])):
        message[...] = s_face[face(up), :]
    for message, up in ((do, place[1]), (de, 1 - place[1])):
        message[pl.ds(0, FACE), :] = t_face[face(up), :]


def inner_kernel(first, work, ylow, yhigh, basis, own_part, own, out, base, plane):
    back_inner(work, ylow, yhigh, basis, out, plane, first)
    base[...] = own[...] * own_part[pl.ds(0, 1), :]


def last_kernel(inner, base, zo, ze, xo, xe, terms, beside, coarse_map, group, top, out):
    place = where_am_i()
    z_low, x_low = place[0] == 0, place[1] == 0
    total = terms[...] + beside[...]
    sums = base[...]
    for at in range(2):
        sums = sums + group[:, at * 128 : (at + 1) * 128] * terms[pl.ds(4 + at, 1), :]
    for at in range(4):
        sums = sums + top[:, at * 128 : (at + 1) * 128] * total[at : at + 1]
    sol = jnp.sum(sums, axis=1, keepdims=True)
    hit = lax.broadcasted_iota(jnp.int32, (128, 128), 0) == coarse_map[pl.ds(0, 1), :]
    out[...] = inner[...] + jnp.sum(jnp.where(hit, sol, 0.0), axis=0, keepdims=True)
    out[layer(7), :] += pick(z_low, ze, zo, 0, FACE)
    out[layer(0), :] += pick(z_low, zo, ze, 0, FACE)
    above = keep(place[3], pick(x_low, xe, xo, 0, FACE))
    below = keep(place[2], pick(x_low, xo, xe, 0, FACE))
    for k in range(8):
        out[pl.ds(k * 64 + 56, 8), :] += above[k * 8 : k * 8 + 8]
        out[pl.ds(k * 64, 8), :] += below[k * 8 : k * 8 + 8]


def move(value, axis, pairs):
    return lax.ppermute(value, axis, pairs)


def body(residual, margin, diag, basis, eigen, coarse_map, own, group, top):
    shape = residual.shape
    residual, margin, diag = (a.reshape(-1, 128) for a in (residual, margin, diag))
    basis, eigen = (a.reshape(-1, 1, 128) for a in (basis, eigen))
    coarse_map = coarse_map.reshape(1, 128)
    own, group, top = (a.reshape(128, -1) for a in (own, group, top))
    doms, coarses = lax.axis_size("dom"), lax.axis_size("coarse")
    z_even, z_odd = swap(doms, 1, 0), swap(doms, 1, 1)
    x_even, x_odd = swap(coarses, 1, 0), swap(coarses, 1, 1)
    inner_rows = (840, 160, 160)

    both = [(i, i ^ (coarses + 1)) for i in range(doms * coarses)]
    is_top = jnp.arange(8)[:, None] < 4
    held = [jax.ShapeDtypeStruct(a.shape, a.dtype) for a in (coarse_map, own, group, top)]

    zo, ze, xe, xo, w, c2, terms, own_part, coarse_map, own, group, top = call(
        first_kernel, [128, 136, 136, 128, 512, 512, 8, 8] + held, (512,) * 3,
        residual, margin, diag, coarse_map, own, group, top,
        in_hbm=range(7), scratch=[pltpu.SemaphoreType.DMA((7,))], flops=300000,
    )
    azo, aze = move(zo, "dom", z_odd), move(ze, "dom", z_even)
    axe, axo = move(xe, "coarse", x_even), move(xo, "coarse", x_odd)
    across = move(terms, ("dom", "coarse"), both)
    work, ylow, yhigh, inverse, terms = call(
        own_kernel, inner_rows + (1040, 8), (128, 104), w, basis, eigen, terms, flops=20000000
    )
    terms = terms + axe[128:] + jnp.where(is_top, aze[128:] + across, 0.0)
    beside = move(terms, "coarse", swap(coarses, 4, 0))
    zo, ze, xo, xe, r, z_face, x_face = call(
        pass_kernel, (LINK + 8, LINK, 128, 128, 512, 128, 128), (FACE,) * 4 + inner_rows + (128,),
        w, c2, azo, aze, axo, axe, basis, work, ylow, yhigh, inverse,
    )
    terms = terms + beside
    zo = move(lax.dynamic_update_slice(zo, terms, (LINK, 0)), "dom", z_odd)
    ze, xe, xo = move(ze, "dom", z_even), move(xe, "coarse", x_even), move(xo, "coarse", x_odd)
    terms = terms + jnp.where(is_top, zo[LINK:], 0.0)
    wide = jnp.concatenate([terms, jnp.zeros((32, 128), F32)])
    terms = terms + jnp.where(is_top, move(wide, "dom", swap(doms, 4, 0))[:8], 0.0)
    ro, re = call(relay_kernel, (RELAY, RELAY), (), zo, ze, flops=1000)
    re, ro = move(re, "coarse", x_even), move(ro, "coarse", x_odd)
    beside = move(terms, "dom", swap(doms, 8, 0))
    first, work, ylow, yhigh = call(
        second_own_kernel, (512,) + inner_rows, (512, 128), w, c2, r, zo, ze, xo, xe, basis, flops=1000
    )
    co, ce, do, de, work, ylow, yhigh = call(
        second_pass_kernel, (FACE, FACE, FACE + 8, FACE) + inner_rows, (FACE,) * 4 + (128,) * 2,
        azo, aze, axo, axe, z_face, x_face, zo, ze, xo, xe, ro, re, basis, work, ylow, yhigh, inverse,
    )
    terms = terms + jnp.where(is_top, beside, 0.0)
    xo = move(lax.dynamic_update_slice(do, terms, (FACE, 0)), "coarse", x_odd)
    zo, ze, xe = move(co, "dom", z_odd), move(ce, "dom", z_even), move(de, "coarse", x_even)
    terms = terms + xo[FACE:]
    beside = move(terms, "dom", swap(doms, 8, 1))
    inner, base = call(inner_kernel, (512, 128), (128,), first, work, ylow, yhigh, basis, own_part, own, flops=1000)
    (out,) = call(last_kernel, (512,), (), inner, base, zo, ze, xo, xe, terms, beside, coarse_map, group, top, flops=300000)
    return out.reshape(shape)


def solution(mesh):
    field = P(None, None, None, "dom", "coarse", None)
    factor = P("dom", "coarse", None, None)
    in_specs = (field, field, field, field, P(None, None, "dom", "coarse", None), P("dom", "coarse", None))
    in_specs = in_specs + (factor, factor, factor)
    return jax.shard_map(body, mesh=mesh, in_specs=in_specs, out_specs=field, check_vma=False)
```

```python
import jax
import jax.numpy as jnp
from jax import lax
from jax.experimental import pallas as pl
from jax.experimental.pallas import tpu as pltpu
from jax.sharding import PartitionSpec as P

sum_scale = 0.015625
F32 = jnp.float32
FACE = 64
LINK = 144
RELAY = 32
VMEM = pl.BlockSpec(memory_space=pltpu.VMEM)


def where_am_i():
    dom, coarse = lax.axis_index("dom"), lax.axis_index("coarse")
    last = lax.axis_size("coarse") - 1
    return dom % 2, coarse % 2, (coarse > 0).astype(jnp.int32), (coarse < last).astype(jnp.int32)


def swap(length, stride, odd):
    ring = length // stride
    pairs = []
    for low in range(odd, ring, 2):
        high = (low + 1) % ring
        pairs += [(low, high), (high, low)]
    return [(a * stride + r, b * stride + r) for a, b in pairs for r in range(stride)]


def within(length, group, odd):
    pairs = swap(group, 1, odd)
    return [(base + a, base + b) for base in range(0, length, group) for a, b in pairs]


def call(kernel, outs, scratch_rows, *args, in_hbm=(), scratch=(), flops=2 * 60000 * 128):
    outs = [jax.ShapeDtypeStruct((out, 128), F32) if isinstance(out, int) else out for out in outs]
    specs = [VMEM] * len(args)
    args = list(args)
    for at in in_hbm:
        specs[at] = pl.BlockSpec(memory_space=pltpu.HBM)
        args[at] = pltpu.with_memory_space_constraint(args[at], pltpu.HBM)
    return pl.pallas_call(
        kernel,
        out_shape=outs,
        in_specs=specs,
        out_specs=[VMEM] * len(outs),
        scratch_shapes=[pltpu.VMEM((rows, 128), F32) for rows in scratch_rows] + list(scratch),
        compiler_params=pltpu.CompilerParams(vmem_limit_bytes=8 * 1024 * 1024),
        cost_estimate=pl.CostEstimate(flops=flops, bytes_accessed=1000000, transcendentals=0),
    )(*args)


def rows8(start):
    return pl.ds(pl.multiple_of(start, 8), 8)


def every(start, stride):
    return pl.ds(start, 8, stride=stride)


def weigh(basis, direction, inputs, first_in, outs, forward):
    results = []
    for out in outs:
        total = None
        for at, tiles in enumerate(inputs):
            pair = (first_in + at, out) if forward else (out, first_in + at)
            coef = basis[direction * 100 + pair[0] * 10 + pair[1]]
            terms = [coef * tile for tile in tiles]
            total = terms if total is None else [a + b for a, b in zip(total, terms)]
        results.append(total)
    return results


ALL_TEN = range(10)
INNER = range(1, 9)


def forward_own(field, basis, work, ylow, yhigh, plane):
    def y_face_in(face, at, turn):
        lines = [[pltpu.roll(field[every(k * 64 + at, 8), :], turn, 1)] for k in range(8)]
        for k, (value,) in enumerate(weigh(basis, 0, lines, 1, ALL_TEN, True)):
            plane[rows8(k * 8), :] = value
        lines = [[plane[every(i, 8), :], plane[every(64 + i, 8), :]] for i in range(8)]
        for i, (value, rest) in enumerate(weigh(basis, 1, lines, 1, ALL_TEN, True)):
            face[every(i, 10), :] = value
            face[every(80 + i, 10), :] = rest

    y_face_in(ylow, 7, 1)
    y_face_in(yhigh, 0, 127)

    def forward_z(step, carry):
        tiles = [step * 2, step * 2 + 1]
        lines = [[field[rows8(k * 64 + i * 8), :] for i in tiles] for k in range(8)]
        for k, values in enumerate(weigh(basis, 0, lines, 1, ALL_TEN, True)):
            for i, value in zip(tiles, values):
                work[rows8((k * 10 + i + 1) * 8), :] = value
        return carry

    lax.fori_loop(0, 4, forward_z, 0)


def solve(work_in, ylow_in, yhigh_in, z_low, z_high, x_low, x_high, basis, inverse, work, ylow, yhigh):
    def add_z(step, carry):
        tiles = [step * 2, step * 2 + 1]
        low = [z_low[rows8(i * 8), :] for i in tiles]
        high = [z_high[rows8(i * 8), :] for i in tiles]
        for k in ALL_TEN:
            for i, a, b in zip(tiles, low, high):
                rows = rows8((k * 10 + i + 1) * 8)
                work[rows, :] = work_in[rows, :] + basis[k] * a + basis[90 + k] * b
        return carry

    lax.fori_loop(0, 4, add_z, 0)
    lines = [[x_low[rows8(k * 8), :], x_high[rows8(k * 8), :]] for k in range(8)]
    for k, (low, high) in enumerate(weigh(basis, 0, lines, 1, ALL_TEN, True)):
        work[rows8(k * 80), :] = low
        work[rows8(k * 80 + 72), :] = high

    def turn_x(forward):
        def step_x(step, carry):
            ks = [step * 2, step * 2 + 1]
            lines = [[work[rows8(k * 80 + i * 8), :] for k in ks] for i in range(10)]
            for i, values in enumerate(weigh(basis, 1, lines, 0, ALL_TEN, forward)):
                for k, value in zip(ks, values):
                    work[rows8(k * 80 + i * 8), :] = value
            return carry

        lax.fori_loop(0, 5, step_x, 0)

    turn_x(True)

    def step_y(step, carry):
        rows = rows8(step * 8)
        lines = [[ylow_in[rows, :]]] + [[work[every(step * 64 + j, 8), :]] for j in range(8)] + [[yhigh_in[rows, :]]]
        spectral = weigh(basis, 2, lines, 0, ALL_TEN, True)
        spectral = [[value * inverse[rows8(j * 104 + step * 8), :]] for j, (value,) in enumerate(spectral)]
        solved = weigh(basis, 2, spectral, 0, ALL_TEN, False)
        ylow[rows, :] = solved[0][0]
        yhigh[rows, :] = solved[9][0]
        for j in range(8):
            work[every(step * 64 + j, 8), :] = solved[j + 1][0]
        return carry

    lax.fori_loop(0, 13, step_y, 0)
    turn_x(False)


def back_faces(work, basis, z_face, x_face):
    def back_z(step, carry):
        tiles = [step * 2, step * 2 + 1]
        lines = [[work[rows8((k * 10 + i + 1) * 8), :] for i in tiles] for k in range(10)]
        for at, values in enumerate(weigh(basis, 0, lines, 0, (0, 9), False)):
            for i, value in zip(tiles, values):
                z_face[rows8(at * FACE + i * 8), :] = value
        return carry

    lax.fori_loop(0, 4, back_z, 0)
    lines = [[work[rows8(k * 80), :], work[rows8(k * 80 + 72), :]] for k in range(10)]
    for k, (low, high) in enumerate(weigh(basis, 0, lines, 0, INNER, False)):
        x_face[rows8(k * 8), :] = low
        x_face[rows8(FACE + k * 8), :] = high


def back_inner(work, ylow, yhigh, basis, out, plane, plus=None):
    def back_z(step, carry):
        tiles = [step * 2, step * 2 + 1]
        lines = [[work[rows8((k * 10 + i + 1) * 8), :] for i in tiles] for k in range(10)]
        for k, values in enumerate(weigh(basis, 0, lines, 0, INNER, False)):
            for i, value in zip(tiles, values):
                rows = rows8(k * 64 + i * 8)
                out[rows, :] = value if plus is None else value + plus[rows, :]
        return carry

    lax.fori_loop(0, 4, back_z, 0)

    def y_face_out(face, at, turn):
        lines = [[face[every(i, 10), :], face[every(80 + i, 10), :]] for i in range(10)]
        for i, (value, rest) in enumerate(weigh(basis, 1, lines, 0, INNER, False)):
            plane[rows8(i * 16), :] = value
            plane[rows8(i * 16 + 8), :] = rest
        lines = [[plane[every(k, 16), :]] for k in range(10)]
        for k, (value,) in enumerate(weigh(basis, 0, lines, 0, INNER, False)):
            out[every(k * 64 + at, 8), :] += pltpu.roll(value, turn, 1)

    y_face_out(ylow, 7, 127)
    y_face_out(yhigh, 0, 1)


def layer(k):
    return pl.ds(pl.multiple_of(k * 64, 64), 64)


def face(at):
    return pl.ds(pl.multiple_of(at * FACE, FACE), FACE)


def put_x(ref, base, array, i):
    for k in range(8):
        ref[pl.ds(base + k * 8, 8), :] = array[rows8(k * 64 + i * 8), :]


def pick(flag, array, other, start, rows):
    return jnp.where(flag, array[pl.ds(start, rows), :], other[pl.ds(start, rows), :])


def keep(flag, value):
    return jnp.where(flag == 1, value, 0.0)


def first_kernel(
    residual_hbm, margin_hbm, diag_hbm, map_hbm, own_hbm, group_hbm, top_hbm,
    zo, ze, xe, xo, w, c2, terms, own_part, coarse_map, own, group, top, residual, margin, diag, sems
):
    place = where_am_i()
    sources = (residual_hbm, margin_hbm, diag_hbm, map_hbm, own_hbm, group_hbm, top_hbm)
    targets = (residual, margin, diag, coarse_map, own, group, top)
    copies = [pltpu.make_async_copy(a, b, sems.at[at]) for at, (a, b) in enumerate(zip(sources, targets))]
    for copy in copies:
        copy.start()
    copies[0].wait()
    copies[1].wait()
    w[...] = margin[...] * residual[...]
    copies[2].wait()
    c2[...] = margin[...] * diag[...]
    z_up, x_up = place[0], place[1]
    for base, source in ((0, w), (FACE, c2)):
        zo[pl.ds(base, FACE), :] = source[layer(z_up * 7), :]
        ze[pl.ds(base, FACE), :] = source[layer(7 - z_up * 7), :]
        put_x(xo, base, source, x_up * 7)
        put_x(xe, base, source, 7 - x_up * 7)
    total = w[pl.ds(0, 8), :]
    for at in range(8, 512, 8):
        total = total + w[pl.ds(at, 8), :]
    element_sum = jnp.sum(total, axis=0, keepdims=True) * sum_scale
    for copy in copies[3:]:
        copy.wait()
    hit = lax.broadcasted_iota(jnp.int32, (128, 128), 0) == coarse_map[pl.ds(0, 1), :]
    rhs = jnp.sum(jnp.where(hit, element_sum, 0.0), axis=1, keepdims=True)
    own_part[...] = jnp.zeros((8, 128), F32)
    own_part[pl.ds(0, 1), :] = jnp.sum(own[...] * rhs, axis=0, keepdims=True)
    terms[...] = jnp.zeros((8, 128), F32)
    for at in range(4):
        terms[pl.ds(at, 1), :] = jnp.sum(top[:, at * 128 : (at + 1) * 128] * rhs, axis=0, keepdims=True)
    for at in range(2):
        terms[pl.ds(4 + at, 1), :] = jnp.sum(group[:, at * 128 : (at + 1) * 128] * rhs, axis=0, keepdims=True)
    ze[pl.ds(128, 8), :] = terms[...]
    xe[pl.ds(128, 8), :] = terms[...]


def own_kernel(w, basis, eigen, terms, work, ylow, yhigh, inverse, same, plane, zx):
    same[...] = terms[...]
    forward_own(w, basis, work, ylow, yhigh, plane)
    for k in range(10):
        for i in range(10):
            zx[pl.ds(k * 10 + i, 1), :] = eigen[k] + eigen[10 + i]
    for j in range(10):
        inverse[pl.ds(j * 104, 104), :] = 1.0 / (zx[...] + eigen[20 + j])


def pass_kernel(
    azo, terms, aze, axe, axo, w, c2, basis, work_in, ylow_in, yhigh_in, inverse,
    zo, ze, xo, xe, r, z_face, x_face, zl, zh, xl, xh, work, ylow, yhigh, plane
):
    place = where_am_i()
    z_low, x_low = place[0] == 0, place[1] == 0
    zh[...] = pick(z_low, aze, azo, 0, FACE)
    zl[...] = pick(z_low, azo, aze, 0, FACE)
    xh[...] = keep(place[3], pick(x_low, axe, axo, 0, FACE))
    xl[...] = keep(place[2], pick(x_low, axo, axe, 0, FACE))
    solve(work_in, ylow_in, yhigh_in, zl, zh, xl, xh, basis, inverse, work, ylow, yhigh)
    back_faces(work, basis, z_face, x_face)
    back_inner(work, ylow, yhigh, basis, r, plane)
    for message, up in ((zo, place[0]), (ze, 1 - place[0])):
        here = layer(up * 7)
        message[pl.ds(0, FACE), :] = z_face[face(up), :]
        message[pl.ds(FACE, FACE), :] = w[here, :] - c2[here, :] * r[here, :]
        message[pl.ds(128, 8), :] = x_face[rows8(FACE + up * 56), :]
        message[pl.ds(136, 8), :] = x_face[rows8(up * 56), :]
    for message, up in ((xo, place[1]), (xe, 1 - place[1])):
        message[pl.ds(0, FACE), :] = x_face[face(up), :]
        for k in range(8):
            here = rows8(k * 64 + up * 56)
            message[pl.ds(FACE + k * 8, 8), :] = w[here, :] - c2[here, :] * r[here, :]


def relay_kernel(zo, ze, xo, xe, ro, re):
    place = where_am_i()
    z_low = place[0] == 0
    for message, up in ((ro, place[1]), (re, 1 - place[1])):
        edge = rows8(136 - up * 8)
        line = rows8(up * 56)
        message[pl.ds(0, 8), :] = jnp.where(z_low, zo[edge, :], ze[edge, :])
        message[pl.ds(8, 8), :] = jnp.where(z_low, ze[edge, :], zo[edge, :])
        message[pl.ds(16, 8), :] = jnp.where(z_low, zo[line, :], ze[line, :])
        message[pl.ds(24, 8), :] = jnp.where(z_low, ze[line, :], zo[line, :])


def second_own_kernel(w, c2, r, zo, ze, xo, xe, basis, first, work, ylow, yhigh, field, plane):
    place = where_am_i()
    z_low, x_low = place[0] == 0, place[1] == 0
    first[...] = r[...]
    first[layer(7), :] += pick(z_low, ze, zo, 0, FACE)
    first[layer(0), :] += pick(z_low, zo, ze, 0, FACE)
    above = keep(place[3], pick(x_low, xe, xo, 0, FACE))
    below = keep(place[2], pick(x_low, xo, xe, 0, FACE))
    for k in range(8):
        first[pl.ds(k * 64 + 56, 8), :] += above[k * 8 : k * 8 + 8]
        first[pl.ds(k * 64, 8), :] += below[k * 8 : k * 8 + 8]
    field[...] = w[...] - c2[...] * first[...]
    forward_own(field, basis, work, ylow, yhigh, plane)


def second_pass_kernel(
    azo, aze, axo, axe, z_face, x_face, zo, ze, xo, xe, ro, re, basis, work_in, ylow_in, yhigh_in, inverse,
    co, ce, do, de, work, ylow, yhigh, zl, zh, xl, xh, s_face, t_face
):
    place = where_am_i()
    z_low, x_low = place[0] == 0, place[1] == 0
    above = keep(place[3], pick(x_low, re, ro, 0, RELAY))
    below = keep(place[2], pick(x_low, ro, re, 0, RELAY))
    for halo, start, edge in ((zl, 0, 0), (zh, FACE, 8)):
        halo[...] = z_face[pl.ds(start, FACE), :]
        halo[pl.ds(0, 8), :] += below[edge : edge + 8]
        halo[pl.ds(56, 8), :] += above[edge : edge + 8]
    for halo, start, edges in ((xl, 0, below), (xh, FACE, above)):
        halo[...] = x_face[pl.ds(start, FACE), :]
        halo[pl.ds(0, 8), :] += edges[16:24]
        halo[pl.ds(56, 8), :] += edges[24:32]
    zh[...] = pick(z_low, ze, zo, FACE, FACE) - pick(z_low, aze, azo, FACE, FACE) * zh[...]
    zl[...] = pick(z_low, zo, ze, FACE, FACE) - pick(z_low, azo, aze, FACE, FACE) * zl[...]
    xh[...] = keep(place[3], pick(x_low, xe, xo, FACE, FACE) - pick(x_low, axe, axo, FACE, FACE) * xh[...])
    xl[...] = keep(place[2], pick(x_low, xo, xe, FACE, FACE) - pick(x_low, axo, axe, FACE, FACE) * xl[...])
    solve(work_in, ylow_in, yhigh_in, zl, zh, xl, xh, basis, inverse, work, ylow, yhigh)
    back_faces(work, basis, s_face, t_face)
    for message, up in ((co, place[0]), (ce, 1 - place[0])):
        message[...] = s_face[face(up), :]
    for message, up in ((do, place[1]), (de, 1 - place[1])):
        message[pl.ds(0, FACE), :] = t_face[face(up), :]


def inner_kernel(first, work, ylow, yhigh, basis, own_part, own, out, base, plane):
    back_inner(work, ylow, yhigh, basis, out, plane, first)
    base[...] = own[...] * own_part[pl.ds(0, 1), :]


def last_kernel(inner, base, zo, ze, xo, terms, beside, xe, coarse_map, group, top, out):
    place = where_am_i()
    z_low, x_low = place[0] == 0, place[1] == 0
    total = terms[...] + beside[...]
    sums = base[...]
    for at in range(2):
        sums = sums + group[:, at * 128 : (at + 1) * 128] * terms[pl.ds(4 + at, 1), :]
    for at in range(4):
        sums = sums + top[:, at * 128 : (at + 1) * 128] * total[at : at + 1]
    sol = jnp.sum(sums, axis=1, keepdims=True)
    hit = lax.broadcasted_iota(jnp.int32, (128, 128), 0) == coarse_map[pl.ds(0, 1), :]
    out[...] = inner[...] + jnp.sum(jnp.where(hit, sol, 0.0), axis=0, keepdims=True)
    out[layer(7), :] += pick(z_low, ze, zo, 0, FACE)
    out[layer(0), :] += pick(z_low, zo, ze, 0, FACE)
    above = keep(place[3], pick(x_low, xe, xo, 0, FACE))
    below = keep(place[2], pick(x_low, xo, xe, 0, FACE))
    for k in range(8):
        out[pl.ds(k * 64 + 56, 8), :] += above[k * 8 : k * 8 + 8]
        out[pl.ds(k * 64, 8), :] += below[k * 8 : k * 8 + 8]


def move(value, axis, pairs):
    return lax.ppermute(value, axis, pairs)


def body(residual, margin, diag, basis, eigen, coarse_map, own, group, top):
    shape = residual.shape
    residual, margin, diag = (a.reshape(-1, 128) for a in (residual, margin, diag))
    basis, eigen = (a.reshape(-1, 1, 128) for a in (basis, eigen))
    coarse_map = coarse_map.reshape(1, 128)
    own, group, top = (a.reshape(128, -1) for a in (own, group, top))
    doms, coarses = lax.axis_size("dom"), lax.axis_size("coarse")
    z_even, z_odd = swap(doms, 1, 0), swap(doms, 1, 1)
    x_even, x_odd = swap(coarses, 1, 0), swap(coarses, 1, 1)
    inner_rows = (840, 160, 160)

    both = [(i, i ^ (coarses + 1)) for i in range(doms * coarses)]
    is_top = jnp.arange(8)[:, None] < 4
    held = [jax.ShapeDtypeStruct(a.shape, a.dtype) for a in (coarse_map, own, group, top)]

    zo, ze, xe, xo, w, c2, terms, own_part, coarse_map, own, group, top = call(
        first_kernel, [128, 136, 136, 128, 512, 512, 8, 8] + held, (512,) * 3,
        residual, margin, diag, coarse_map, own, group, top,
        in_hbm=range(7), scratch=[pltpu.SemaphoreType.DMA((7,))], flops=300000,
    )
    azo, aze = move(zo, "dom", z_odd), move(ze, "dom", z_even)
    axe, axo = move(xe, "coarse", x_even), move(xo, "coarse", x_odd)
    across = move(terms, ("dom", "coarse"), both)
    work, ylow, yhigh, inverse, terms = call(
        own_kernel, inner_rows + (1040, 8), (128, 104), w, basis, eigen, terms, flops=20000000
    )
    terms = terms + axe[128:] + jnp.where(is_top, aze[128:] + across, 0.0)
    beside = move(terms, "coarse", swap(coarses, 4, 0))
    zo, ze, xo, xe, r, z_face, x_face = call(
        pass_kernel, (LINK + 8, LINK, 128, 128, 512, 128, 128), (FACE,) * 4 + inner_rows + (128,),
        azo, terms, aze, axe, axo, w, c2, basis, work, ylow, yhigh, inverse,
    )
    terms = terms + beside
    zo = move(lax.dynamic_update_slice(zo, terms, (LINK, 0)), "dom", z_odd)
    ze, xe, xo = move(ze, "dom", z_even), move(xe, "coarse", x_even), move(xo, "coarse", x_odd)
    terms = terms + jnp.where(is_top, zo[LINK:], 0.0)
    wide = jnp.concatenate([terms, jnp.zeros((32, 128), F32)])
    terms = terms + jnp.where(is_top, move(wide, "dom", swap(doms, 4, 0))[:8], 0.0)
    ro, re = call(relay_kernel, (RELAY, RELAY), (), zo, ze, xo, xe, flops=1000)
    re, ro = move(re, "coarse", x_even), move(ro, "coarse", x_odd)
    beside = move(terms, "dom", swap(doms, 8, 0))
    first, work, ylow, yhigh = call(
        second_own_kernel, (512,) + inner_rows, (512, 128), w, c2, r, zo, ze, xo, xe, basis, flops=1000
    )
    co, ce, do, de, work, ylow, yhigh = call(
        second_pass_kernel, (FACE, FACE, FACE + 8, FACE) + inner_rows, (FACE,) * 4 + (128,) * 2,
        azo, aze, axo, axe, z_face, x_face, zo, ze, xo, xe, ro, re, basis, work, ylow, yhigh, inverse,
    )
    terms = terms + jnp.where(is_top, beside, 0.0)
    xo = move(lax.dynamic_update_slice(do, terms, (FACE, 0)), "coarse", x_odd)
    zo, ze, xe = move(co, "dom", z_odd), move(ce, "dom", z_even), move(de, "coarse", x_even)
    terms = terms + xo[FACE:]
    beside = move(terms, "dom", swap(doms, 8, 1))
    inner, base = call(inner_kernel, (512, 128), (128,), first, work, ylow, yhigh, basis, own_part, own, flops=1000)
    (out,) = call(last_kernel, (512,), (), inner, base, zo, ze, xo, terms, beside, xe, coarse_map, group, top, flops=300000)
    return out.reshape(shape)


def solution(mesh):
    field = P(None, None, None, "dom", "coarse", None)
    factor = P("dom", "coarse", None, None)
    in_specs = (field, field, field, field, P(None, None, "dom", "coarse", None), P("dom", "coarse", None))
    in_specs = in_specs + (factor, factor, factor)
    return jax.shard_map(body, mesh=mesh, in_specs=in_specs, out_specs=field, check_vma=False)
```

```python
import jax
import jax.numpy as jnp
from jax import lax
from jax.experimental import pallas as pl
from jax.experimental.pallas import tpu as pltpu
from jax.sharding import PartitionSpec as P

sum_scale = 0.015625
F32 = jnp.float32
FACE = 64
LINK = 144
RELAY = 32
VMEM = pl.BlockSpec(memory_space=pltpu.VMEM)


def where_am_i():
    dom, coarse = lax.axis_index("dom"), lax.axis_index("coarse")
    last = lax.axis_size("coarse") - 1
    return dom % 2, coarse % 2, (coarse > 0).astype(jnp.int32), (coarse < last).astype(jnp.int32)


def swap(length, stride, odd):
    ring = length // stride
    pairs = []
    for low in range(odd, ring, 2):
        high = (low + 1) % ring
        pairs += [(low, high), (high, low)]
    return [(a * stride + r, b * stride + r) for a, b in pairs for r in range(stride)]


def within(length, group, odd):
    pairs = swap(group, 1, odd)
    return [(base + a, base + b) for base in range(0, length, group) for a, b in pairs]


def call(kernel, outs, scratch_rows, *args, in_hbm=(), scratch=(), flops=2 * 60000 * 128):
    outs = [jax.ShapeDtypeStruct((out, 128), F32) if isinstance(out, int) else out for out in outs]
    specs = [VMEM] * len(args)
    args = list(args)
    for at in in_hbm:
        specs[at] = pl.BlockSpec(memory_space=pltpu.HBM)
        args[at] = pltpu.with_memory_space_constraint(args[at], pltpu.HBM)
    return pl.pallas_call(
        kernel,
        out_shape=outs,
        in_specs=specs,
        out_specs=[VMEM] * len(outs),
        scratch_shapes=[pltpu.VMEM((rows, 128), F32) for rows in scratch_rows] + list(scratch),
        compiler_params=pltpu.CompilerParams(vmem_limit_bytes=8 * 1024 * 1024),
        cost_estimate=pl.CostEstimate(flops=flops, bytes_accessed=1000000, transcendentals=0),
    )(*args)


def rows8(start):
    return pl.ds(pl.multiple_of(start, 8), 8)


def every(start, stride):
    return pl.ds(start, 8, stride=stride)


def weigh(basis, direction, inputs, first_in, outs, forward):
    results = []
    for out in outs:
        total = None
        for at, tiles in enumerate(inputs):
            pair = (first_in + at, out) if forward else (out, first_in + at)
            coef = basis[direction * 100 + pair[0] * 10 + pair[1]]
            terms = [coef * tile for tile in tiles]
            total = terms if total is None else [a + b for a, b in zip(total, terms)]
        results.append(total)
    return results


ALL_TEN = range(10)
INNER = range(1, 9)


def forward_own(field, basis, work, ylow, yhigh, plane):
    def y_face_in(face, at, turn):
        lines = [[pltpu.roll(field[every(k * 64 + at, 8), :], turn, 1)] for k in range(8)]
        for k, (value,) in enumerate(weigh(basis, 0, lines, 1, ALL_TEN, True)):
            plane[rows8(k * 8), :] = value
        lines = [[plane[every(i, 8), :], plane[every(64 + i, 8), :]] for i in range(8)]
        for i, (value, rest) in enumerate(weigh(basis, 1, lines, 1, ALL_TEN, True)):
            face[every(i, 10), :] = value
            face[every(80 + i, 10), :] = rest

    y_face_in(ylow, 7, 1)
    y_face_in(yhigh, 0, 127)

    def forward_z(step, carry):
        tiles = [step * 2, step * 2 + 1]
        lines = [[field[rows8(k * 64 + i * 8), :] for i in tiles] for k in range(8)]
        for k, values in enumerate(weigh(basis, 0, lines, 1, ALL_TEN, True)):
            for i, value in zip(tiles, values):
                work[rows8((k * 10 + i + 1) * 8), :] = value
        return carry

    lax.fori_loop(0, 4, forward_z, 0)


def solve(work_in, ylow_in, yhigh_in, z_low, z_high, x_low, x_high, basis, inverse, work, ylow, yhigh):
    def add_z(step, carry):
        tiles = [step * 2, step * 2 + 1]
        low = [z_low[rows8(i * 8), :] for i in tiles]
        high = [z_high[rows8(i * 8), :] for i in tiles]
        for k in ALL_TEN:
            for i, a, b in zip(tiles, low, high):
                rows = rows8((k * 10 + i + 1) * 8)
                work[rows, :] = work_in[rows, :] + basis[k] * a + basis[90 + k] * b
        return carry

    lax.fori_loop(0, 4, add_z, 0)
    lines = [[x_low[rows8(k * 8), :], x_high[rows8(k * 8), :]] for k in range(8)]
    for k, (low, high) in enumerate(weigh(basis, 0, lines, 1, ALL_TEN, True)):
        work[rows8(k * 80), :] = low
        work[rows8(k * 80 + 72), :] = high

    def turn_x(forward):
        def step_x(step, carry):
            ks = [step * 2, step * 2 + 1]
            lines = [[work[rows8(k * 80 + i * 8), :] for k in ks] for i in range(10)]
            for i, values in enumerate(weigh(basis, 1, lines, 0, ALL_TEN, forward)):
                for k, value in zip(ks, values):
                    work[rows8(k * 80 + i * 8), :] = value
            return carry

        lax.fori_loop(0, 5, step_x, 0)

    turn_x(True)

    def step_y(step, carry):
        rows = rows8(step * 8)
        lines = [[ylow_in[rows, :]]] + [[work[every(step * 64 + j, 8), :]] for j in range(8)] + [[yhigh_in[rows, :]]]
        spectral = weigh(basis, 2, lines, 0, ALL_TEN, True)
        spectral = [[value * inverse[rows8(j * 104 + step * 8), :]] for j, (value,) in enumerate(spectral)]
        solved = weigh(basis, 2, spectral, 0, ALL_TEN, False)
        ylow[rows, :] = solved[0][0]
        yhigh[rows, :] = solved[9][0]
        for j in range(8):
            work[every(step * 64 + j, 8), :] = solved[j + 1][0]
        return carry

    lax.fori_loop(0, 13, step_y, 0)
    turn_x(False)


def back_faces(work, basis, z_face, x_face):
    def back_z(step, carry):
        tiles = [step * 2, step * 2 + 1]
        lines = [[work[rows8((k * 10 + i + 1) * 8), :] for i in tiles] for k in range(10)]
        for at, values in enumerate(weigh(basis, 0, lines, 0, (0, 9), False)):
            for i, value in zip(tiles, values):
                z_face[rows8(at * FACE + i * 8), :] = value
        return carry

    lax.fori_loop(0, 4, back_z, 0)
    lines = [[work[rows8(k * 80), :], work[rows8(k * 80 + 72), :]] for k in range(10)]
    for k, (low, high) in enumerate(weigh(basis, 0, lines, 0, INNER, False)):
        x_face[rows8(k * 8), :] = low
        x_face[rows8(FACE + k * 8), :] = high


def back_inner(work, ylow, yhigh, basis, out, plane, plus=None):
    def back_z(step, carry):
        tiles = [step * 2, step * 2 + 1]
        lines = [[work[rows8((k * 10 + i + 1) * 8), :] for i in tiles] for k in range(10)]
        for k, values in enumerate(weigh(basis, 0, lines, 0, INNER, False)):
            for i, value in zip(tiles, values):
                rows = rows8(k * 64 + i * 8)
                out[rows, :] = value if plus is None else value + plus[rows, :]
        return carry

    lax.fori_loop(0, 4, back_z, 0)

    def y_face_out(face, at, turn):
        lines = [[face[every(i, 10), :], face[every(80 + i, 10), :]] for i in range(10)]
        for i, (value, rest) in enumerate(weigh(basis, 1, lines, 0, INNER, False)):
            plane[rows8(i * 16), :] = value
            plane[rows8(i * 16 + 8), :] = rest
        lines = [[plane[every(k, 16), :]] for k in range(10)]
        for k, (value,) in enumerate(weigh(basis, 0, lines, 0, INNER, False)):
            out[every(k * 64 + at, 8), :] += pltpu.roll(value, turn, 1)

    y_face_out(ylow, 7, 127)
    y_face_out(yhigh, 0, 1)


def layer(k):
    return pl.ds(pl.multiple_of(k * 64, 64), 64)


def face(at):
    return pl.ds(pl.multiple_of(at * FACE, FACE), FACE)


def put_x(ref, base, array, i):
    for k in range(8):
        ref[pl.ds(base + k * 8, 8), :] = array[rows8(k * 64 + i * 8), :]


def pick(flag, array, other, start, rows):
    return jnp.where(flag, array[pl.ds(start, rows), :], other[pl.ds(start, rows), :])


def keep(flag, value):
    return jnp.where(flag == 1, value, 0.0)


def first_kernel(
    residual_hbm, margin_hbm, diag_hbm, map_hbm, own_hbm, group_hbm, top_hbm,
    zo, ze, xe, xo, w, c2, terms, own_part, coarse_map, own, group, top, residual, margin, diag, sems
):
    place = where_am_i()
    sources = (residual_hbm, margin_hbm, diag_hbm, map_hbm, own_hbm, group_hbm, top_hbm)
    targets = (residual, margin, diag, coarse_map, own, group, top)
    copies = [pltpu.make_async_copy(a, b, sems.at[at]) for at, (a, b) in enumerate(zip(sources, targets))]
    for copy in copies:
        copy.start()
    copies[0].wait()
    copies[1].wait()
    w[...] = margin[...] * residual[...]
    copies[2].wait()
    c2[...] = margin[...] * diag[...]
    z_up, x_up = place[0], place[1]
    for base, source in ((0, w), (FACE, c2)):
        zo[pl.ds(base, FACE), :] = source[layer(z_up * 7), :]
        ze[pl.ds(base, FACE), :] = source[layer(7 - z_up * 7), :]
        put_x(xo, base, source, x_up * 7)
        put_x(xe, base, source, 7 - x_up * 7)
    total = w[pl.ds(0, 8), :]
    for at in range(8, 512, 8):
        total = total + w[pl.ds(at, 8), :]
    element_sum = jnp.sum(total, axis=0, keepdims=True) * sum_scale
    for copy in copies[3:]:
        copy.wait()
    hit = lax.broadcasted_iota(jnp.int32, (128, 128), 0) == coarse_map[pl.ds(0, 1), :]
    rhs = jnp.sum(jnp.where(hit, element_sum, 0.0), axis=1, keepdims=True)
    own_part[...] = jnp.zeros((8, 128), F32)
    own_part[pl.ds(0, 1), :] = jnp.sum(own[...] * rhs, axis=0, keepdims=True)
    terms[...] = jnp.zeros((8, 128), F32)
    for at in range(4):
        terms[pl.ds(at, 1), :] = jnp.sum(top[:, at * 128 : (at + 1) * 128] * rhs, axis=0, keepdims=True)
    for at in range(2):
        terms[pl.ds(4 + at, 1), :] = jnp.sum(group[:, at * 128 : (at + 1) * 128] * rhs, axis=0, keepdims=True)
    ze[pl.ds(128, 8), :] = terms[...]
    xe[pl.ds(128, 8), :] = terms[...]


def own_kernel(w, basis, eigen, terms, work, ylow, yhigh, inverse, same, plane, zx):
    same[...] = terms[...]
    forward_own(w, basis, work, ylow, yhigh, plane)
    for k in range(10):
        for i in range(10):
            zx[pl.ds(k * 10 + i, 1), :] = eigen[k] + eigen[10 + i]
    for j in range(10):
        inverse[pl.ds(j * 104, 104), :] = 1.0 / (zx[...] + eigen[20 + j])


def pass_kernel(
    azo, terms, aze, axe, axo, w, c2, basis, work_in, ylow_in, yhigh_in, inverse,
    zo, ze, xo, xe, r, z_face, x_face, zl, zh, xl, xh, work, ylow, yhigh, plane
):
    place = where_am_i()
    z_low, x_low = place[0] == 0, place[1] == 0
    zh[...] = pick(z_low, aze, azo, 0, FACE)
    zl[...] = pick(z_low, azo, aze, 0, FACE)
    xh[...] = keep(place[3], pick(x_low, axe, axo, 0, FACE))
    xl[...] = keep(place[2], pick(x_low, axo, axe, 0, FACE))
    solve(work_in, ylow_in, yhigh_in, zl, zh, xl, xh, basis, inverse, work, ylow, yhigh)
    back_faces(work, basis, z_face, x_face)
    back_inner(work, ylow, yhigh, basis, r, plane)
    for message, up in ((zo, place[0]), (ze, 1 - place[0])):
        here = layer(up * 7)
        message[pl.ds(0, FACE), :] = z_face[face(up), :]
        message[pl.ds(FACE, FACE), :] = w[here, :] - c2[here, :] * r[here, :]
        message[pl.ds(128, 8), :] = x_face[rows8(FACE + up * 56), :]
        message[pl.ds(136, 8), :] = x_face[rows8(up * 56), :]
    for message, up in ((xo, place[1]), (xe, 1 - place[1])):
        message[pl.ds(0, FACE), :] = x_face[face(up), :]
        for k in range(8):
            here = rows8(k * 64 + up * 56)
            message[pl.ds(FACE + k * 8, 8), :] = w[here, :] - c2[here, :] * r[here, :]


def relay_kernel(zo, ze, xo, xe, ro, re):
    place = where_am_i()
    z_low = place[0] == 0
    for message, up in ((ro, place[1]), (re, 1 - place[1])):
        edge = rows8(136 - up * 8)
        line = rows8(up * 56)
        message[pl.ds(0, 8), :] = jnp.where(z_low, zo[edge, :], ze[edge, :])
        message[pl.ds(8, 8), :] = jnp.where(z_low, ze[edge, :], zo[edge, :])
        message[pl.ds(16, 8), :] = jnp.where(z_low, zo[line, :], ze[line, :])
        message[pl.ds(24, 8), :] = jnp.where(z_low, ze[line, :], zo[line, :])


def second_own_kernel(w, c2, r, zo, ze, xo, xe, basis, first, work, ylow, yhigh, field, plane):
    place = where_am_i()
    z_low, x_low = place[0] == 0, place[1] == 0
    first[...] = r[...]
    first[layer(7), :] += pick(z_low, ze, zo, 0, FACE)
    first[layer(0), :] += pick(z_low, zo, ze, 0, FACE)
    above = keep(place[3], pick(x_low, xe, xo, 0, FACE))
    below = keep(place[2], pick(x_low, xo, xe, 0, FACE))
    for k in range(8):
        first[pl.ds(k * 64 + 56, 8), :] += above[k * 8 : k * 8 + 8]
        first[pl.ds(k * 64, 8), :] += below[k * 8 : k * 8 + 8]
    field[...] = w[...] - c2[...] * first[...]
    forward_own(field, basis, work, ylow, yhigh, plane)


def second_pass_kernel(
    azo, aze, axo, axe, z_face, x_face, zo, ze, xo, xe, ro, re, basis, work_in, ylow_in, yhigh_in, inverse,
    co, ce, do, de, work, ylow, yhigh, zl, zh, xl, xh, s_face, t_face
):
    place = where_am_i()
    z_low, x_low = place[0] == 0, place[1] == 0
    above = keep(place[3], pick(x_low, re, ro, 0, RELAY))
    below = keep(place[2], pick(x_low, ro, re, 0, RELAY))
    for halo, start, edge in ((zl, 0, 0), (zh, FACE, 8)):
        halo[...] = z_face[pl.ds(start, FACE), :]
        halo[pl.ds(0, 8), :] += below[edge : edge + 8]
        halo[pl.ds(56, 8), :] += above[edge : edge + 8]
    for halo, start, edges in ((xl, 0, below), (xh, FACE, above)):
        halo[...] = x_face[pl.ds(start, FACE), :]
        halo[pl.ds(0, 8), :] += edges[16:24]
        halo[pl.ds(56, 8), :] += edges[24:32]
    zh[...] = pick(z_low, ze, zo, FACE, FACE) - pick(z_low, aze, azo, FACE, FACE) * zh[...]
    zl[...] = pick(z_low, zo, ze, FACE, FACE) - pick(z_low, azo, aze, FACE, FACE) * zl[...]
    xh[...] = keep(place[3], pick(x_low, xe, xo, FACE, FACE) - pick(x_low, axe, axo, FACE, FACE) * xh[...])
    xl[...] = keep(place[2], pick(x_low, xo, xe, FACE, FACE) - pick(x_low, axo, axe, FACE, FACE) * xl[...])
    solve(work_in, ylow_in, yhigh_in, zl, zh, xl, xh, basis, inverse, work, ylow, yhigh)
    back_faces(work, basis, s_face, t_face)
    for message, up in ((co, place[0]), (ce, 1 - place[0])):
        message[...] = s_face[face(up), :]
    for message, up in ((do, place[1]), (de, 1 - place[1])):
        message[pl.ds(0, FACE), :] = t_face[face(up), :]


def inner_kernel(first, work, ylow, yhigh, basis, own_part, own, out, base, plane):
    back_inner(work, ylow, yhigh, basis, out, plane, first)
    base[...] = own[...] * own_part[pl.ds(0, 1), :]


def correct(sums, coarse_map):
    sol = jnp.sum(sums, axis=1, keepdims=True)
    hit = lax.broadcasted_iota(jnp.int32, (128, 128), 0) == coarse_map[pl.ds(0, 1), :]
    return jnp.sum(jnp.where(hit, sol, 0.0), axis=0, keepdims=True)


def add_top(sums, top, total):
    for at in range(4):
        product = top[:, at * 128 : (at + 1) * 128] * total[pl.ds(at, 1), :]
        sums = product if sums is None else sums + product
    return sums


def gather_kernel(inner, base, zo, ze, xo, xe, terms, coarse_map, group, top, out):
    place = where_am_i()
    z_low, x_low = place[0] == 0, place[1] == 0
    sums = base[...]
    for at in range(2):
        sums = sums + group[:, at * 128 : (at + 1) * 128] * terms[pl.ds(4 + at, 1), :]
    out[...] = inner[...] + correct(add_top(sums, top, terms), coarse_map)
    out[layer(7), :] += pick(z_low, ze, zo, 0, FACE)
    out[layer(0), :] += pick(z_low, zo, ze, 0, FACE)
    above = keep(place[3], pick(x_low, xe, xo, 0, FACE))
    below = keep(place[2], pick(x_low, xo, xe, 0, FACE))
    for k in range(8):
        out[pl.ds(k * 64 + 56, 8), :] += above[k * 8 : k * 8 + 8]
        out[pl.ds(k * 64, 8), :] += below[k * 8 : k * 8 + 8]


def last_kernel(gathered, beside, coarse_map, top, out):
    out[...] = gathered[...] + correct(add_top(None, top, beside), coarse_map)


def move(value, axis, pairs):
    return lax.ppermute(value, axis, pairs)


def body(residual, margin, diag, basis, eigen, coarse_map, own, group, top):
    shape = residual.shape
    residual, margin, diag = (a.reshape(-1, 128) for a in (residual, margin, diag))
    basis, eigen = (a.reshape(-1, 1, 128) for a in (basis, eigen))
    coarse_map = coarse_map.reshape(1, 128)
    own, group, top = (a.reshape(128, -1) for a in (own, group, top))
    doms, coarses = lax.axis_size("dom"), lax.axis_size("coarse")
    z_even, z_odd = swap(doms, 1, 0), swap(doms, 1, 1)
    x_even, x_odd = swap(coarses, 1, 0), swap(coarses, 1, 1)
    inner_rows = (840, 160, 160)

    both = [(i, i ^ (coarses + 1)) for i in range(doms * coarses)]
    is_top = jnp.arange(8)[:, None] < 4
    held = [jax.ShapeDtypeStruct(a.shape, a.dtype) for a in (coarse_map, own, group, top)]

    zo, ze, xe, xo, w, c2, terms, own_part, coarse_map, own, group, top = call(
        first_kernel, [128, 136, 136, 128, 512, 512, 8, 8] + held, (512,) * 3,
        residual, margin, diag, coarse_map, own, group, top,
        in_hbm=range(7), scratch=[pltpu.SemaphoreType.DMA((7,))], flops=300000,
    )
    azo, aze = move(zo, "dom", z_odd), move(ze, "dom", z_even)
    axe, axo = move(xe, "coarse", x_even), move(xo, "coarse", x_odd)
    across = move(terms, ("dom", "coarse"), both)
    work, ylow, yhigh, inverse, terms = call(
        own_kernel, inner_rows + (1040, 8), (128, 104), w, basis, eigen, terms, flops=20000000
    )
    terms = terms + axe[128:] + jnp.where(is_top, aze[128:] + across, 0.0)
    beside = move(terms, "coarse", swap(coarses, 4, 0))
    zo, ze, xo, xe, r, z_face, x_face = call(
        pass_kernel, (LINK + 8, LINK, 128, 128, 512, 128, 128), (FACE,) * 4 + inner_rows + (128,),
        azo, terms, aze, axe, axo, w, c2, basis, work, ylow, yhigh, inverse,
    )
    terms = terms + beside
    zo = move(lax.dynamic_update_slice(zo, terms, (LINK, 0)), "dom", z_odd)
    ze, xe, xo = move(ze, "dom", z_even), move(xe, "coarse", x_even), move(xo, "coarse", x_odd)
    terms = terms + jnp.where(is_top, zo[LINK:], 0.0)
    wide = jnp.concatenate([terms, jnp.zeros((32, 128), F32)])
    terms = terms + jnp.where(is_top, move(wide, "dom", swap(doms, 8, 0))[:8], 0.0)
    ro, re = call(relay_kernel, (RELAY, RELAY), (), zo, ze, xo, xe, flops=1000)
    re, ro = move(re, "coarse", x_even), move(ro, "coarse", x_odd)
    beside = move(terms, "dom", swap(doms, 8, 1))
    first, work, ylow, yhigh = call(
        second_own_kernel, (512,) + inner_rows, (512, 128), w, c2, r, zo, ze, xo, xe, basis, flops=1000
    )
    co, ce, do, de, work, ylow, yhigh = call(
        second_pass_kernel, (FACE, FACE, FACE + 8, FACE) + inner_rows, (FACE,) * 4 + (128,) * 2,
        azo, aze, axo, axe, z_face, x_face, zo, ze, xo, xe, ro, re, basis, work, ylow, yhigh, inverse,
    )
    terms = terms + jnp.where(is_top, beside, 0.0)
    xo = move(lax.dynamic_update_slice(do, terms, (FACE, 0)), "coarse", x_odd)
    zo, ze, xe = move(co, "dom", z_odd), move(ce, "dom", z_even), move(de, "coarse", x_even)
    terms = terms + xo[FACE:]
    beside = move(terms, "dom", swap(doms, 4, 0))
    inner, base = call(inner_kernel, (512, 128), (128,), first, work, ylow, yhigh, basis, own_part, own, flops=1000)
    (gathered,) = call(gather_kernel, (512,), (), inner, base, zo, ze, xo, xe, terms, coarse_map, group, top, flops=1000)
    (out,) = call(last_kernel, (512,), (), gathered, beside, coarse_map, top, flops=1000)
    return out.reshape(shape)


def solution(mesh):
    field = P(None, None, None, "dom", "coarse", None)
    factor = P("dom", "coarse", None, None)
    in_specs = (field, field, field, field, P(None, None, "dom", "coarse", None), P("dom", "coarse", None))
    in_specs = in_specs + (factor, factor, factor)
    return jax.shard_map(body, mesh=mesh, in_specs=in_specs, out_specs=field, check_vma=False)
```

```python
import jax
import jax.numpy as jnp
from jax import lax
from jax.experimental import pallas as pl
from jax.experimental.pallas import tpu as pltpu
from jax.sharding import PartitionSpec as P

sum_scale = 0.015625
F32 = jnp.float32
FACE = 64
LINK = 144
RELAY = 32
VMEM = pl.BlockSpec(memory_space=pltpu.VMEM)


def where_am_i():
    dom, coarse = lax.axis_index("dom"), lax.axis_index("coarse")
    last = lax.axis_size("coarse") - 1
    return dom % 2, coarse % 2, (coarse > 0).astype(jnp.int32), (coarse < last).astype(jnp.int32)


def swap(length, stride, odd):
    ring = length // stride
    pairs = []
    for low in range(odd, ring, 2):
        high = (low + 1) % ring
        pairs += [(low, high), (high, low)]
    return [(a * stride + r, b * stride + r) for a, b in pairs for r in range(stride)]


def within(length, group, odd):
    pairs = swap(group, 1, odd)
    return [(base + a, base + b) for base in range(0, length, group) for a, b in pairs]


def call(kernel, outs, scratch_rows, *args, in_hbm=(), scratch=(), flops=2 * 60000 * 128):
    outs = [jax.ShapeDtypeStruct((out, 128), F32) if isinstance(out, int) else out for out in outs]
    specs = [VMEM] * len(args)
    args = list(args)
    for at in in_hbm:
        specs[at] = pl.BlockSpec(memory_space=pltpu.HBM)
        args[at] = pltpu.with_memory_space_constraint(args[at], pltpu.HBM)
    return pl.pallas_call(
        kernel,
        out_shape=outs,
        in_specs=specs,
        out_specs=[VMEM] * len(outs),
        scratch_shapes=[pltpu.VMEM((rows, 128), F32) for rows in scratch_rows] + list(scratch),
        compiler_params=pltpu.CompilerParams(vmem_limit_bytes=8 * 1024 * 1024),
        cost_estimate=pl.CostEstimate(flops=flops, bytes_accessed=1000000, transcendentals=0),
    )(*args)


def rows8(start):
    return pl.ds(pl.multiple_of(start, 8), 8)


def every(start, stride):
    return pl.ds(start, 8, stride=stride)


def weigh(basis, direction, inputs, first_in, outs, forward):
    results = []
    for out in outs:
        total = None
        for at, tiles in enumerate(inputs):
            pair = (first_in + at, out) if forward else (out, first_in + at)
            coef = basis[direction * 100 + pair[0] * 10 + pair[1]]
            terms = [coef * tile for tile in tiles]
            total = terms if total is None else [a + b for a, b in zip(total, terms)]
        results.append(total)
    return results


ALL_TEN = range(10)
INNER = range(1, 9)


def forward_own(field, basis, work, ylow, yhigh, plane):
    def y_face_in(face, at, turn):
        lines = [[pltpu.roll(field[every(k * 64 + at, 8), :], turn, 1)] for k in range(8)]
        for k, (value,) in enumerate(weigh(basis, 0, lines, 1, ALL_TEN, True)):
            plane[rows8(k * 8), :] = value
        lines = [[plane[every(i, 8), :], plane[every(64 + i, 8), :]] for i in range(8)]
        for i, (value, rest) in enumerate(weigh(basis, 1, lines, 1, ALL_TEN, True)):
            face[every(i, 10), :] = value
            face[every(80 + i, 10), :] = rest

    y_face_in(ylow, 7, 1)
    y_face_in(yhigh, 0, 127)

    def forward_z(step, carry):
        tiles = [step * 2, step * 2 + 1]
        lines = [[field[rows8(k * 64 + i * 8), :] for i in tiles] for k in range(8)]
        for k, values in enumerate(weigh(basis, 0, lines, 1, ALL_TEN, True)):
            for i, value in zip(tiles, values):
                work[rows8((k * 10 + i + 1) * 8), :] = value
        return carry

    lax.fori_loop(0, 4, forward_z, 0)


def solve(work_in, ylow_in, yhigh_in, z_low, z_high, x_low, x_high, basis, inverse, work, ylow, yhigh):
    def add_z(step, carry):
        tiles = [step * 2, step * 2 + 1]
        low = [z_low[rows8(i * 8), :] for i in tiles]
        high = [z_high[rows8(i * 8), :] for i in tiles]
        for k in ALL_TEN:
            for i, a, b in zip(tiles, low, high):
                rows = rows8((k * 10 + i + 1) * 8)
                work[rows, :] = work_in[rows, :] + basis[k] * a + basis[90 + k] * b
        return carry

    lax.fori_loop(0, 4, add_z, 0)
    lines = [[x_low[rows8(k * 8), :], x_high[rows8(k * 8), :]] for k in range(8)]
    for k, (low, high) in enumerate(weigh(basis, 0, lines, 1, ALL_TEN, True)):
        work[rows8(k * 80), :] = low
        work[rows8(k * 80 + 72), :] = high

    def turn_x(forward):
        def step_x(step, carry):
            ks = [step * 2, step * 2 + 1]
            lines = [[work[rows8(k * 80 + i * 8), :] for k in ks] for i in range(10)]
            for i, values in enumerate(weigh(basis, 1, lines, 0, ALL_TEN, forward)):
                for k, value in zip(ks, values):
                    work[rows8(k * 80 + i * 8), :] = value
            return carry

        lax.fori_loop(0, 5, step_x, 0)

    turn_x(True)

    def step_y(step, carry):
        rows = rows8(step * 8)
        lines = [[ylow_in[rows, :]]] + [[work[every(step * 64 + j, 8), :]] for j in range(8)] + [[yhigh_in[rows, :]]]
        spectral = weigh(basis, 2, lines, 0, ALL_TEN, True)
        spectral = [[value * inverse[rows8(j * 104 + step * 8), :]] for j, (value,) in enumerate(spectral)]
        solved = weigh(basis, 2, spectral, 0, ALL_TEN, False)
        ylow[rows, :] = solved[0][0]
        yhigh[rows, :] = solved[9][0]
        for j in range(8):
            work[every(step * 64 + j, 8), :] = solved[j + 1][0]
        return carry

    lax.fori_loop(0, 13, step_y, 0)
    turn_x(False)


def back_faces(work, basis, z_face, x_face):
    def back_z(step, carry):
        tiles = [step * 2, step * 2 + 1]
        lines = [[work[rows8((k * 10 + i + 1) * 8), :] for i in tiles] for k in range(10)]
        for at, values in enumerate(weigh(basis, 0, lines, 0, (0, 9), False)):
            for i, value in zip(tiles, values):
                z_face[rows8(at * FACE + i * 8), :] = value
        return carry

    lax.fori_loop(0, 4, back_z, 0)
    lines = [[work[rows8(k * 80), :], work[rows8(k * 80 + 72), :]] for k in range(10)]
    for k, (low, high) in enumerate(weigh(basis, 0, lines, 0, INNER, False)):
        x_face[rows8(k * 8), :] = low
        x_face[rows8(FACE + k * 8), :] = high


def back_inner(work, ylow, yhigh, basis, out, plane, plus=None):
    def back_z(step, carry):
        tiles = [step * 2, step * 2 + 1]
        lines = [[work[rows8((k * 10 + i + 1) * 8), :] for i in tiles] for k in range(10)]
        for k, values in enumerate(weigh(basis, 0, lines, 0, INNER, False)):
            for i, value in zip(tiles, values):
                rows = rows8(k * 64 + i * 8)
                out[rows, :] = value if plus is None else value + plus[rows, :]
        return carry

    lax.fori_loop(0, 4, back_z, 0)

    def y_face_out(face, at, turn):
        lines = [[face[every(i, 10), :], face[every(80 + i, 10), :]] for i in range(10)]
        for i, (value, rest) in enumerate(weigh(basis, 1, lines, 0, INNER, False)):
            plane[rows8(i * 16), :] = value
            plane[rows8(i * 16 + 8), :] = rest
        lines = [[plane[every(k, 16), :]] for k in range(10)]
        for k, (value,) in enumerate(weigh(basis, 0, lines, 0, INNER, False)):
            out[every(k * 64 + at, 8), :] += pltpu.roll(value, turn, 1)

    y_face_out(ylow, 7, 127)
    y_face_out(yhigh, 0, 1)


def layer(k):
    return pl.ds(pl.multiple_of(k * 64, 64), 64)


def face(at):
    return pl.ds(pl.multiple_of(at * FACE, FACE), FACE)


def put_x(ref, base, array, i):
    for k in range(8):
        ref[pl.ds(base + k * 8, 8), :] = array[rows8(k * 64 + i * 8), :]


def pick(flag, array, other, start, rows):
    return jnp.where(flag, array[pl.ds(start, rows), :], other[pl.ds(start, rows), :])


def keep(flag, value):
    return jnp.where(flag == 1, value, 0.0)


def first_kernel(
    residual_hbm, margin_hbm, diag_hbm, map_hbm, own_hbm, group_hbm, top_hbm,
    zo, ze, xe, xo, w, c2, terms, own_part, coarse_map, own, group, top, residual, margin, diag, sems
):
    place = where_am_i()
    sources = (residual_hbm, margin_hbm, diag_hbm, map_hbm, own_hbm, group_hbm, top_hbm)
    targets = (residual, margin, diag, coarse_map, own, group, top)
    copies = [pltpu.make_async_copy(a, b, sems.at[at]) for at, (a, b) in enumerate(zip(sources, targets))]
    for copy in copies:
        copy.start()
    copies[0].wait()
    copies[1].wait()
    w[...] = margin[...] * residual[...]
    copies[2].wait()
    c2[...] = margin[...] * diag[...]
    z_up, x_up = place[0], place[1]
    for base, source in ((0, w), (FACE, c2)):
        zo[pl.ds(base, FACE), :] = source[layer(z_up * 7), :]
        ze[pl.ds(base, FACE), :] = source[layer(7 - z_up * 7), :]
        put_x(xo, base, source, x_up * 7)
        put_x(xe, base, source, 7 - x_up * 7)
    total = w[pl.ds(0, 8), :]
    for at in range(8, 512, 8):
        total = total + w[pl.ds(at, 8), :]
    element_sum = jnp.sum(total, axis=0, keepdims=True) * sum_scale
    for copy in copies[3:]:
        copy.wait()
    hit = lax.broadcasted_iota(jnp.int32, (128, 128), 0) == coarse_map[pl.ds(0, 1), :]
    rhs = jnp.sum(jnp.where(hit, element_sum, 0.0), axis=1, keepdims=True)
    own_part[...] = jnp.zeros((8, 128), F32)
    own_part[pl.ds(0, 1), :] = jnp.sum(own[...] * rhs, axis=0, keepdims=True)
    terms[...] = jnp.zeros((8, 128), F32)
    for at in range(4):
        terms[pl.ds(at, 1), :] = jnp.sum(top[:, at * 128 : (at + 1) * 128] * rhs, axis=0, keepdims=True)
    for at in range(2):
        terms[pl.ds(4 + at, 1), :] = jnp.sum(group[:, at * 128 : (at + 1) * 128] * rhs, axis=0, keepdims=True)
    ze[pl.ds(128, 8), :] = terms[...]
    xe[pl.ds(128, 8), :] = terms[...]


def own_kernel(w, basis, eigen, terms, work, ylow, yhigh, inverse, same, plane, zx):
    same[...] = terms[...]
    forward_own(w, basis, work, ylow, yhigh, plane)
    for k in range(10):
        for i in range(10):
            zx[pl.ds(k * 10 + i, 1), :] = eigen[k] + eigen[10 + i]
    for j in range(10):
        inverse[pl.ds(j * 104, 104), :] = 1.0 / (zx[...] + eigen[20 + j])


def pass_kernel(
    azo, terms, aze, axe, axo, w, c2, basis, work_in, ylow_in, yhigh_in, inverse,
    zo, ze, xo, xe, r, z_face, x_face, zl, zh, xl, xh, work, ylow, yhigh, plane
):
    place = where_am_i()
    z_low, x_low = place[0] == 0, place[1] == 0
    zh[...] = pick(z_low, aze, azo, 0, FACE)
    zl[...] = pick(z_low, azo, aze, 0, FACE)
    xh[...] = keep(place[3], pick(x_low, axe, axo, 0, FACE))
    xl[...] = keep(place[2], pick(x_low, axo, axe, 0, FACE))
    solve(work_in, ylow_in, yhigh_in, zl, zh, xl, xh, basis, inverse, work, ylow, yhigh)
    back_faces(work, basis, z_face, x_face)
    back_inner(work, ylow, yhigh, basis, r, plane)
    for message, up in ((zo, place[0]), (ze, 1 - place[0])):
        here = layer(up * 7)
        message[pl.ds(0, FACE), :] = z_face[face(up), :]
        message[pl.ds(FACE, FACE), :] = w[here, :] - c2[here, :] * r[here, :]
        message[pl.ds(128, 8), :] = x_face[rows8(FACE + up * 56), :]
        message[pl.ds(136, 8), :] = x_face[rows8(up * 56), :]
    for message, up in ((xo, place[1]), (xe, 1 - place[1])):
        message[pl.ds(0, FACE), :] = x_face[face(up), :]
        for k in range(8):
            here = rows8(k * 64 + up * 56)
            message[pl.ds(FACE + k * 8, 8), :] = w[here, :] - c2[here, :] * r[here, :]


def relay_kernel(zo, ze, xo, xe, ro, re):
    place = where_am_i()
    z_low = place[0] == 0
    for message, up in ((ro, place[1]), (re, 1 - place[1])):
        edge = rows8(136 - up * 8)
        line = rows8(up * 56)
        message[pl.ds(0, 8), :] = jnp.where(z_low, zo[edge, :], ze[edge, :])
        message[pl.ds(8, 8), :] = jnp.where(z_low, ze[edge, :], zo[edge, :])
        message[pl.ds(16, 8), :] = jnp.where(z_low, zo[line, :], ze[line, :])
        message[pl.ds(24, 8), :] = jnp.where(z_low, ze[line, :], zo[line, :])


def second_own_kernel(w, c2, r, zo, ze, xo, xe, basis, first, work, ylow, yhigh, field, plane):
    place = where_am_i()
    z_low, x_low = place[0] == 0, place[1] == 0
    first[...] = r[...]
    first[layer(7), :] += pick(z_low, ze, zo, 0, FACE)
    first[layer(0), :] += pick(z_low, zo, ze, 0, FACE)
    above = keep(place[3], pick(x_low, xe, xo, 0, FACE))
    below = keep(place[2], pick(x_low, xo, xe, 0, FACE))
    for k in range(8):
        first[pl.ds(k * 64 + 56, 8), :] += above[k * 8 : k * 8 + 8]
        first[pl.ds(k * 64, 8), :] += below[k * 8 : k * 8 + 8]
    field[...] = w[...] - c2[...] * first[...]
    forward_own(field, basis, work, ylow, yhigh, plane)


def second_pass_kernel(
    azo, aze, axo, axe, z_face, x_face, zo, ze, xo, xe, ro, re, basis, work_in, ylow_in, yhigh_in, inverse,
    co, ce, do, de, work, ylow, yhigh, zl, zh, xl, xh, s_face, t_face
):
    place = where_am_i()
    z_low, x_low = place[0] == 0, place[1] == 0
    above = keep(place[3], pick(x_low, re, ro, 0, RELAY))
    below = keep(place[2], pick(x_low, ro, re, 0, RELAY))
    for halo, start, edge in ((zl, 0, 0), (zh, FACE, 8)):
        halo[...] = z_face[pl.ds(start, FACE), :]
        halo[pl.ds(0, 8), :] += below[edge : edge + 8]
        halo[pl.ds(56, 8), :] += above[edge : edge + 8]
    for halo, start, edges in ((xl, 0, below), (xh, FACE, above)):
        halo[...] = x_face[pl.ds(start, FACE), :]
        halo[pl.ds(0, 8), :] += edges[16:24]
        halo[pl.ds(56, 8), :] += edges[24:32]
    zh[...] = pick(z_low, ze, zo, FACE, FACE) - pick(z_low, aze, azo, FACE, FACE) * zh[...]
    zl[...] = pick(z_low, zo, ze, FACE, FACE) - pick(z_low, azo, aze, FACE, FACE) * zl[...]
    xh[...] = keep(place[3], pick(x_low, xe, xo, FACE, FACE) - pick(x_low, axe, axo, FACE, FACE) * xh[...])
    xl[...] = keep(place[2], pick(x_low, xo, xe, FACE, FACE) - pick(x_low, axo, axe, FACE, FACE) * xl[...])
    solve(work_in, ylow_in, yhigh_in, zl, zh, xl, xh, basis, inverse, work, ylow, yhigh)
    back_faces(work, basis, s_face, t_face)
    for message, up in ((co, place[0]), (ce, 1 - place[0])):
        message[...] = s_face[face(up), :]
    for message, up in ((do, place[1]), (de, 1 - place[1])):
        message[pl.ds(0, FACE), :] = t_face[face(up), :]


def inner_kernel(first, work, ylow, yhigh, basis, own_part, own, out, base, plane):
    back_inner(work, ylow, yhigh, basis, out, plane, first)
    base[...] = own[...] * own_part[pl.ds(0, 1), :]


def correct(sums, coarse_map):
    sol = jnp.sum(sums, axis=1, keepdims=True)
    hit = lax.broadcasted_iota(jnp.int32, (128, 128), 0) == coarse_map[pl.ds(0, 1), :]
    return jnp.sum(jnp.where(hit, sol, 0.0), axis=0, keepdims=True)


def add_top(sums, top, total):
    for at in range(4):
        product = top[:, at * 128 : (at + 1) * 128] * total[pl.ds(at, 1), :]
        sums = product if sums is None else sums + product
    return sums


def gather_kernel(inner, base, zo, ze, xo, xe, terms, coarse_map, group, top, out):
    place = where_am_i()
    z_low, x_low = place[0] == 0, place[1] == 0
    sums = base[...]
    for at in range(2):
        sums = sums + group[:, at * 128 : (at + 1) * 128] * terms[pl.ds(4 + at, 1), :]
    out[...] = inner[...] + correct(add_top(sums, top, terms), coarse_map)
    out[layer(7), :] += pick(z_low, ze, zo, 0, FACE)
    out[layer(0), :] += pick(z_low, zo, ze, 0, FACE)
    above = keep(place[3], pick(x_low, xe, xo, 0, FACE))
    below = keep(place[2], pick(x_low, xo, xe, 0, FACE))
    for k in range(8):
        out[pl.ds(k * 64 + 56, 8), :] += above[k * 8 : k * 8 + 8]
        out[pl.ds(k * 64, 8), :] += below[k * 8 : k * 8 + 8]


def last_kernel(gathered, beside, coarse_map, top, out):
    out[...] = gathered[...] + correct(add_top(None, top, beside), coarse_map)


def move(value, axis, pairs):
    return lax.ppermute(value, axis, pairs)


def body(residual, margin, diag, basis, eigen, coarse_map, own, group, top):
    shape = residual.shape
    residual, margin, diag = (a.reshape(-1, 128) for a in (residual, margin, diag))
    basis, eigen = (a.reshape(-1, 1, 128) for a in (basis, eigen))
    coarse_map = coarse_map.reshape(1, 128)
    own, group, top = (a.reshape(128, -1) for a in (own, group, top))
    doms, coarses = lax.axis_size("dom"), lax.axis_size("coarse")
    z_even, z_odd = swap(doms, 1, 0), swap(doms, 1, 1)
    x_even, x_odd = swap(coarses, 1, 0), swap(coarses, 1, 1)
    inner_rows = (840, 160, 160)

    both = [(i, i ^ (coarses + 1)) for i in range(doms * coarses)]
    is_top = jnp.arange(8)[:, None] < 4
    held = [jax.ShapeDtypeStruct(a.shape, a.dtype) for a in (coarse_map, own, group, top)]

    zo, ze, xe, xo, w, c2, terms, own_part, coarse_map, own, group, top = call(
        first_kernel, [128, 136, 136, 128, 512, 512, 8, 8] + held, (512,) * 3,
        residual, margin, diag, coarse_map, own, group, top,
        in_hbm=range(7), scratch=[pltpu.SemaphoreType.DMA((7,))], flops=300000,
    )
    azo, aze = move(zo, "dom", z_odd), move(ze, "dom", z_even)
    axe, axo = move(xe, "coarse", x_even), move(xo, "coarse", x_odd)
    across = move(terms, ("dom", "coarse"), both)
    work, ylow, yhigh, inverse, terms = call(
        own_kernel, inner_rows + (1040, 8), (128, 104), w, basis, eigen, terms, flops=20000000
    )
    terms = terms + axe[128:] + jnp.where(is_top, across + aze[128:], 0.0)
    beside = move(terms, "coarse", swap(coarses, 4, 0))
    zo, ze, xo, xe, r, z_face, x_face = call(
        pass_kernel, (LINK + 8, LINK, 128, 128, 512, 128, 128), (FACE,) * 4 + inner_rows + (128,),
        azo, terms, aze, axe, axo, w, c2, basis, work, ylow, yhigh, inverse,
    )
    terms = terms + beside
    zo = move(lax.dynamic_update_slice(zo, terms, (LINK, 0)), "dom", z_odd)
    ze, xe, xo = move(ze, "dom", z_even), move(xe, "coarse", x_even), move(xo, "coarse", x_odd)
    terms = terms + jnp.where(is_top, zo[LINK:], 0.0)
    wide = jnp.concatenate([terms, jnp.zeros((32, 128), F32)])
    terms = terms + jnp.where(is_top, move(wide, "dom", swap(doms, 4, 0))[:8], 0.0)
    ro, re = call(relay_kernel, (RELAY, RELAY), (), zo, ze, xo, xe, flops=1000)
    re, ro = move(re, "coarse", x_even), move(ro, "coarse", x_odd)
    beside = move(terms, "dom", swap(doms, 8, 0))
    first, work, ylow, yhigh = call(
        second_own_kernel, (512,) + inner_rows, (512, 128), w, c2, r, zo, ze, xo, xe, basis, flops=1000
    )
    co, ce, do, de, work, ylow, yhigh = call(
        second_pass_kernel, (FACE, FACE, FACE + 8, FACE) + inner_rows, (FACE,) * 4 + (128,) * 2,
        azo, aze, axo, axe, z_face, x_face, zo, ze, xo, xe, ro, re, basis, work, ylow, yhigh, inverse,
    )
    terms = terms + jnp.where(is_top, beside, 0.0)
    xo = move(lax.dynamic_update_slice(do, terms, (FACE, 0)), "coarse", x_odd)
    zo, ze, xe = move(co, "dom", z_odd), move(ce, "dom", z_even), move(de, "coarse", x_even)
    terms = terms + xo[FACE:]
    beside = move(terms, "dom", swap(doms, 8, 1))
    inner, base = call(inner_kernel, (512, 128), (128,), first, work, ylow, yhigh, basis, own_part, own, flops=1000)
    (gathered,) = call(gather_kernel, (512,), (), inner, base, zo, ze, xo, xe, terms, coarse_map, group, top, flops=1000)
    (out,) = call(last_kernel, (512,), (), gathered, beside, coarse_map, top, flops=1000)
    return out.reshape(shape)


def solution(mesh):
    field = P(None, None, None, "dom", "coarse", None)
    factor = P("dom", "coarse", None, None)
    in_specs = (field, field, field, field, P(None, None, "dom", "coarse", None), P("dom", "coarse", None))
    in_specs = in_specs + (factor, factor, factor)
    return jax.shard_map(body, mesh=mesh, in_specs=in_specs, out_specs=field, check_vma=False)
```
